32 devices in a mesh: cell: 8 (over z, y), own: 4 (over x, core).
Axes of the slice: x: 2, y: 2, z: 4, core: 2. Of those that a mesh axis runs over, the one named last changes fastest.
Arguments:
- hist: bfloat16 [65536, 3, 256], P(('cell', 'own')), as said below
- dest: int32 [65536, 1], P(('cell', 'own')), may hold values from 0 to 31; in each aligned block of 2048 rows (0 to 2047, 2048 to 4095, ...) at most 128 rows name the same one
- cell_in: int32 [65536], P(('cell', 'own')), may hold values from 0 to 1023
- offsets: int32 [4, 32768], P(None, ('cell', 'own')), may hold values from -4 to 4
Outputs:
- multipliers: float32 [2, 6, 32768], P(None, None, ('cell', 'own'))
- fit_stat: float32 [2, 32768], P(None, ('cell', 'own'))
The draws below stay inside these ranges and needn't reach their ends.
Inputs may be any that keep to these rules, and one draw needn't show every extreme that they name: `dest`: the rows of one device name each cell block at most 128 times, and in every draw some device names some block exactly 128 times. `hist`: Positive, every entry at least three ten-thousandths of its row's largest.
All inputs are finite; a program needn't handle non-finite values.
Results may differ from the reference program's by a relative error of at most 0.0022.
Values may be sent and summed in bfloat16 or wider, within the bound.
A program may use at most 64 MiB of HBM per device.

```python
import math
import jax
import jax.numpy as jnp
import numpy as np
from jax import lax

LEV = 128
SPEC = 2
REPL = 3
MOM = 6
NEWTON = 8
NEIGH = 4
W = 4
CB = 1024
ROWS = 2048
NCELL = 32768
ROWS_ALL = 65536
CAP = 128
DEVICES = 32


def draw_hist(key, part):
    key_rate = jax.random.fold_in(key, 11)
    key_rough = jax.random.fold_in(key, 12)
    key_scale = jax.random.fold_in(key, 13)
    log_rate = jax.random.uniform(key_rate, (ROWS_ALL, REPL, SPEC, 1), jnp.float32, jnp.log(0.3), jnp.log(2.5))
    rate = jnp.exp(log_rate)
    xpos = (2.0 * jnp.arange(LEV, dtype=jnp.float32) + 1.0) / LEV - 1.0
    shape = jnp.exp(-rate * (xpos[None, None, None, :] + 1.0))
    rough = jnp.exp(jax.random.uniform(key_rough, (ROWS_ALL, REPL, SPEC, LEV), jnp.float32, jnp.log(1.0 / 3.0), jnp.log(3.0)))
    scale = jnp.exp(jax.random.uniform(key_scale, (ROWS_ALL, 1, 1, 1), jnp.float32, 0.0, jnp.log(10.0)))
    values = shape * rough * scale
    return values.reshape(ROWS_ALL, REPL, SPEC * LEV).astype(jnp.bfloat16)


def place_ends(values, stream_key, smallest, top_value):
    shape = values.shape
    place = [jax.random.randint(jax.random.fold_in(stream_key, axis), (), 0, shape[axis]) for axis in range(len(shape))]
    values = values.at[tuple(place)].set(smallest)
    longest = shape.index(max(shape))
    place[longest] = (place[longest] + 1) % shape[longest]
    return values.at[tuple(place)].set(top_value)


def deal_out(key, own, number, rows, amount, top, reach, slope):
    sequence = jax.random.permutation(key, amount)
    crowded, usual = portions_of(amount, rows * top, reach, slope, True), portions_of(amount, rows * top, reach, slope, False)
    places = jnp.arange(amount)

    def named(tallies, rotation):
        used = int((tallies > 0).sum())
        fixed = max(1, used // 4)
        moved = fixed + (places - fixed + rotation * (used - fixed)) % max(1, amount - fixed)
        return jnp.zeros((amount,), jnp.int32).at[sequence[jnp.where(places < fixed, places, moved)]].set(jnp.asarray(tallies, jnp.int32))

    tallies = jnp.where(number % 4 == 0, named(crowded, number // 4), named(usual, number - number // 4 - 1))
    mixed = jax.random.permutation(jax.random.fold_in(own, 3), amount)
    donor, receiver = mixed[0:amount // 2 * 2:2], mixed[1:amount // 2 * 2:2]
    slack = jnp.minimum(tallies[donor] - 1, reach - tallies[receiver]) // 2
    slack = jnp.where((donor == sequence[0]) | (receiver == sequence[0]) | (tallies[receiver] == 0), 0, jnp.maximum(slack, 0))
    moved = jax.random.randint(jax.random.fold_in(own, 4), (amount // 2,), 0, 1 << 20) % (slack + 1)
    tallies = tallies.at[donor].add(-moved).at[receiver].add(moved)
    items = jnp.searchsorted(jnp.cumsum(tallies), jnp.arange(rows * top), side="right").astype(jnp.int32)
    grid = items.reshape(top, rows).T
    grid = grid[jax.random.permutation(jax.random.fold_in(own, 1), rows)]
    rotation = jax.random.randint(jax.random.fold_in(own, 2), (rows, 1), 0, top)
    return jnp.take_along_axis(grid, (jnp.arange(top)[None, :] + rotation) % top, axis=1)


def portions_of(number_of, total, limit, skew, full):
    loads = [(1 << 20) // math.isqrt(grade ** skew) + 1 for grade in range(1, number_of + 1)]
    largest = limit if full else min(limit, max(-(-total // number_of), total * loads[0] // sum(loads)))
    least = 1 if total - largest >= number_of - 1 else 0
    holding, rest = [largest] + [least] * (number_of - 1), total - largest - least * (number_of - 1)
    while rest > 0:
        free = [i for i in range(1, number_of) if holding[i] < largest] or [i for i in range(1, number_of) if holding[i] < limit]
        whole, remaining = sum([loads[i] for i in free]), rest
        for i in free:
            more = min(limit - holding[i], max(1, remaining * loads[i] // whole), rest)
            holding[i] = holding[i] + more
            rest = rest - more
    return np.array(holding)


def setup_inputs(seed: int = 0) -> dict:
    seeds = jax.random.split(jax.random.key(seed), 5)
    hist = draw_hist(jax.random.fold_in(seeds[4], 71), 0)
    dest_keys = jax.random.split(jax.random.fold_in(seeds[1], 1), ROWS_ALL // ROWS)
    dest_turns = jax.random.permutation(jax.random.fold_in(seeds[1], 3), ROWS_ALL // ROWS)
    dest = jax.vmap(lambda own, number: deal_out(jax.random.fold_in(seeds[1], 2), own, number, ROWS, DEVICES, 1, CAP, 2))(dest_keys, dest_turns).reshape((ROWS_ALL, 1))
    cell_in = place_ends(jax.random.randint(seeds[2], (ROWS_ALL,), 0, CB), jax.random.fold_in(seeds[2], 1), 0, CB - 1).astype(jnp.int32)
    offsets = place_ends(jax.random.randint(seeds[3], (NEIGH, NCELL), 0 - W, W + 1), jax.random.fold_in(seeds[3], 1), 0 - W, W).astype(jnp.int32)
    return dict(hist=hist, dest=dest, cell_in=cell_in, offsets=offsets)


def legendre_table(levels, count):
    xpos = (2.0 * jnp.arange(levels, dtype=jnp.float32) + 1.0) / levels - 1.0
    prev = jnp.ones_like(xpos)
    curr = xpos
    table = [curr]
    for order in range(1, count):
        nxt = ((2 * order + 1) * xpos * curr - order * prev) / (order + 1)
        prev, curr = (curr, nxt)
        table.append(curr)
    return jnp.stack(table, axis=0)

def chol_solve(hess, rhs, count):
    lower = [[None] * count for _ in range(count)]
    for row in range(count):
        for col in range(row + 1):
            total = hess[:, row, col]
            for inner in range(col):
                total = total - lower[row][inner] * lower[col][inner]
            if row == col:
                lower[row][col] = jnp.sqrt(total)
            else:
                lower[row][col] = total / lower[col][col]
    forward = []
    for row in range(count):
        total = rhs[:, row]
        for inner in range(row):
            total = total - lower[row][inner] * forward[inner]
        forward.append(total / lower[row][row])
    backward = [None] * count
    for row in reversed(range(count)):
        total = forward[row]
        for inner in range(row + 1, count):
            total = total - lower[inner][row] * backward[inner]
        backward[row] = total / lower[row][row]
    return jnp.stack(backward, axis=1)

def fit_entropy(target, count, steps):
    spec, levels, cells = target.shape
    hp = lax.Precision.HIGHEST
    phi = legendre_table(levels, count)
    psi = (phi[:, None, :] * phi[None, :, :]).reshape(count * count, levels)
    weights = target / lax.optimization_barrier(jnp.sum(target, axis=1, keepdims=True))
    moments = jnp.einsum('ml,slc->smc', phi, weights, precision=hp)
    lam = jnp.zeros((spec, count, cells), jnp.float32)
    ident = jnp.eye(count, dtype=jnp.float32)[None, :, :, None]
    for step in range(steps):
        expo = jnp.exp(jnp.einsum('ml,smc->slc', phi, lam, precision=hp))
        prob = expo / lax.optimization_barrier(jnp.sum(expo, axis=1, keepdims=True))
        first = jnp.einsum('ml,slc->smc', phi, prob, precision=hp)
        second = jnp.einsum('nl,slc->snc', psi, prob, precision=hp).reshape(spec, count, count, cells)
        hess = second - first[:, :, None, :] * first[:, None, :, :] + 0.01 * ident
        lam = lam - 0.5 * chol_solve(hess, first - moments, count)
    return lam

def fit_statistic(target, lam, count):
    spec, levels, cells = target.shape
    phi = legendre_table(levels, count)
    exponent = jnp.einsum('ml,smc->slc', phi, lam, precision=lax.Precision.HIGHEST)
    log_norm = jnp.log(lax.optimization_barrier(jnp.sum(jnp.exp(exponent), axis=1, keepdims=True)))
    total = lax.optimization_barrier(jnp.sum(target, axis=1, keepdims=True))
    ratio = jnp.log(target / total) - (exponent - log_norm)
    return 2.0 * lax.optimization_barrier(jnp.sum(target * ratio, axis=1)) / levels

def smooth_levels(field):
    padded = jnp.pad(field, ((0, 0), (1, 1), (0, 0)))
    return 0.5 * field + 0.25 * (padded[:, :-2, :] + padded[:, 2:, :])

def reference(hist, dest, cell_in, offsets):
    packed = lax.optimization_barrier(jnp.sum(hist.astype(jnp.float32), axis=1)).astype(jnp.bfloat16)
    cell_id = (dest[:, 0] * CB + cell_in).astype(jnp.int32)
    summed = jax.ops.segment_sum(packed.astype(jnp.float32), cell_id, num_segments=NCELL)
    cellhist = summed.T.reshape(SPEC, LEV, NCELL)
    levelled = smooth_levels(cellhist)
    padded = jnp.pad(levelled, ((0, 0), (0, 0), (W, W)))
    base = jnp.arange(NCELL, dtype=jnp.int32) + W
    target = 1.0 + levelled
    for j in range(NEIGH):
        target = target + jnp.take(padded, (base + offsets[j]).astype(jnp.int32), axis=2)
    lam = fit_entropy(target, MOM, NEWTON)
    return (lam, fit_statistic(target, lam, MOM))
```

```python
import functools
import jax
import jax.numpy as jnp
import numpy as np
from jax import lax
from jax.experimental import pallas as pl
from jax.experimental.pallas import tpu as pltpu
from jax.sharding import PartitionSpec as P

SPEC = 2
MOM = 6
NEWTON = 8
NEIGH = 4
W = 4
TILE = 256
RIM = 8
BF = jnp.bfloat16
F32 = jnp.float32


def legendre_rows(levels, count):
    xpos = (2.0 * np.arange(levels) + 1.0) / levels - 1.0
    table = [np.ones_like(xpos), xpos]
    for order in range(1, count - 1):
        table.append(((2 * order + 1) * xpos * table[order] - order * table[order - 1]) / (order + 1))
    return np.stack(table, axis=0)


def product_weights(count):
    weights = {}
    for m in range(1, count + 1):
        for n in range(1, m + 1):
            series = np.polynomial.legendre.legmul(np.eye(m + 1)[m], np.eye(n + 1)[n])
            weights[m, n] = [(k, float(v)) for k, v in enumerate(series) if abs(v) > 1e-12]
    return weights


def halves(value):
    high = value.astype(BF)
    return high, (value - high.astype(F32)).astype(BF)


def fit_tables(levels):
    rows = np.zeros((16, levels))
    rows[: 2 * MOM + 1] = legendre_rows(levels, 2 * MOM + 1)
    high = np.asarray(rows, jnp.bfloat16)
    low = np.asarray(rows - high.astype(np.float64), jnp.bfloat16)
    gather = np.zeros((32, 2 * levels), jnp.bfloat16)
    gather[:16, :levels] = high
    gather[:16, levels:] = high
    gather[16:, :levels] = low
    spread = np.zeros((levels, 32), jnp.bfloat16)
    spread[:, 0:MOM] = high[1 : MOM + 1].T
    spread[:, 8 : 8 + MOM] = low[1 : MOM + 1].T
    spread[:, 16 : 16 + MOM] = high[1 : MOM + 1].T
    return jnp.asarray(gather), jnp.asarray(spread)


def fit_kernel(cell_ref, low_ref, high_ref, off_ref, gather_ref, spread_ref, lam_ref, stat_ref,
               ext, target, sums, lam, mu):
    cells = cell_ref.shape[0]
    levels = gather_ref.shape[1] // 2
    tiles = cells // TILE
    span = TILE + 2 * RIM
    ext[0:RIM, :] = low_ref[...]
    ext[RIM : RIM + cells, :] = cell_ref[...]
    ext[RIM + cells :, :] = high_ref[...]
    tn = (((0,), (0,)), ((), ()))

    def moments(value):
        high, low = halves(value)
        both = jnp.dot(gather_ref[...], jnp.concatenate([high, low], axis=0), preferred_element_type=F32)
        return both[:16] + both[16:]

    def exponent(group):
        value = lam[:, group, :]
        high = value.astype(BF).astype(F32)
        stacked = jnp.concatenate([high, high, value - high, jnp.zeros_like(high)], axis=0)
        return jnp.dot(spread_ref[...], stacked.astype(BF), preferred_element_type=F32)

    place = lax.broadcasted_iota(jnp.int32, (span, TILE), 0) - lax.broadcasted_iota(jnp.int32, (span, TILE), 1) - RIM
    level = lax.broadcasted_iota(jnp.int32, (levels, TILE), 0)
    for block in range(tiles):
        cols = slice(block * TILE, (block + 1) * TILE)
        picker = (place == 0).astype(F32)
        for j in range(NEIGH):
            picker = picker + (place == off_ref[j : j + 1, cols]).astype(F32)
        picker = picker.astype(BF)
        high, low = halves(ext[block * TILE : block * TILE + span, :])
        summed = lax.dot_general(high, picker, tn, preferred_element_type=F32) + lax.dot_general(
            low, picker, tn, preferred_element_type=F32
        )
        for s in range(SPEC):
            field = summed[s * levels : (s + 1) * levels]
            below = jnp.where(level == 0, 0.0, pltpu.roll(field, 1, 0))
            above = jnp.where(level == levels - 1, 0.0, pltpu.roll(field, levels - 1, 0))
            smooth = 1.0 + (0.5 * field + 0.25 * (below + above))
            group = s * tiles + block
            target[group] = smooth
            sums[:, group, :] = moments(smooth)
    inverse = 1.0 / sums[0]
    for m in range(MOM):
        mu[m] = sums[m + 1] * inverse
    lam[...] = jnp.zeros_like(lam)
    weights = product_weights(MOM)

    def step(_, carry):
        for group in range(SPEC * tiles):
            sums[:, group, :] = moments(jnp.exp(exponent(group)))
        inverse = 1.0 / sums[0]
        mean = [None] + [sums[k] * inverse for k in range(1, 2 * MOM + 1)]
        raw = [[None] * MOM for _ in range(MOM)]
        unit = [[None] * MOM for _ in range(MOM)]
        scale = [None] * MOM
        for row in range(MOM):
            for col in range(row + 1):
                total = -mean[row + 1] * mean[col + 1]
                if row == col:
                    total = total + 0.01
                for k, v in weights[row + 1, col + 1]:
                    total = total + (v if k == 0 else v * mean[k])
                for inner in range(col):
                    total = total - raw[row][inner] * unit[col][inner]
                if row == col:
                    scale[row] = 1.0 / total
                else:
                    raw[row][col] = total
                    unit[row][col] = total * scale[col]
        forward = []
        for row in range(MOM):
            total = mean[row + 1] - mu[row]
            for inner in range(row):
                total = total - unit[row][inner] * forward[inner]
            forward.append(total)
        backward = [None] * MOM
        for row in reversed(range(MOM)):
            total = forward[row] * scale[row]
            for inner in range(row + 1, MOM):
                total = total - unit[inner][row] * backward[inner]
            backward[row] = total
            lam[row] = lam[row] - 0.5 * total
        return carry

    lax.fori_loop(0, NEWTON, step, 0)
    for s in range(SPEC):
        for block in range(tiles):
            cols = slice(block * TILE, (block + 1) * TILE)
            group = s * tiles + block
            lam_ref[s, :, cols] = lam[0:MOM, group, :]
            value = exponent(group)
            norm = jnp.log(jnp.sum(jnp.exp(value), axis=0, keepdims=True))
            field = target[group]
            total = jnp.log(jnp.sum(field, axis=0, keepdims=True))
            ratio = (jnp.log(field) - value) + (norm - total)
            stat_ref[s : s + 1, cols] = (2.0 / levels) * jnp.sum(field * ratio, axis=0, keepdims=True)


def fit(cellhist, low, high, offsets):
    cells, width = cellhist.shape
    levels = width // SPEC
    groups = SPEC * cells // TILE
    gather, spread = fit_tables(levels)
    return pl.pallas_call(
        fit_kernel,
        out_shape=(
            jax.ShapeDtypeStruct((SPEC, MOM, cells), F32),
            jax.ShapeDtypeStruct((SPEC, cells), F32),
        ),
        in_specs=[pl.BlockSpec(memory_space=pltpu.VMEM)] * 6,
        out_specs=(pl.BlockSpec(memory_space=pltpu.VMEM),) * 2,
        scratch_shapes=[
            pltpu.VMEM((cells + 2 * RIM, width), F32),
            pltpu.VMEM((groups, levels, TILE), F32),
            pltpu.VMEM((16, groups, TILE), F32),
            pltpu.VMEM((8, groups, TILE), F32),
            pltpu.VMEM((8, groups, TILE), F32),
        ],
        compiler_params=pltpu.CompilerParams(vmem_limit_bytes=32 * 1024 * 1024),
        name="fit",
    )(cellhist, low, high, offsets, gather, spread)


def body(hist, dest, cell_in, offsets):
    rows = hist.shape[0]
    width = hist.shape[2]
    cells = offsets.shape[1]
    devices = lax.axis_size(("cell", "own"))
    capacity = 2 * rows // devices
    packed = jnp.sum(hist, axis=1, dtype=jnp.float32).astype(jnp.bfloat16)
    target_block = dest[:, 0]
    member = (target_block[:, None] == jnp.arange(devices, dtype=jnp.int32)[None, :]).astype(jnp.int32)
    ranks = jnp.sum((jnp.cumsum(member, axis=0) - 1) * member, axis=1)
    position = target_block * capacity + ranks
    send_rows = jnp.zeros((devices * capacity, width), jnp.bfloat16).at[position].set(packed)
    send_cells = jnp.full((devices * capacity,), -1, jnp.int32).at[position].set(cell_in)
    got_rows = lax.all_to_all(send_rows.reshape(devices, capacity, width), ("cell", "own"), split_axis=0, concat_axis=0, tiled=True)
    got_cells = lax.all_to_all(send_cells.reshape(devices, capacity), ("cell", "own"), split_axis=0, concat_axis=0, tiled=True)
    recv_rows = got_rows.reshape(devices * capacity, width)
    recv_cells = got_cells.reshape(devices * capacity)
    select = (recv_cells[None, :] == jnp.arange(cells, dtype=jnp.int32)[:, None]).astype(jnp.bfloat16)
    cellhist = jnp.dot(select, recv_rows, preferred_element_type=jnp.float32)
    forward = [(i, i + 1) for i in range(devices - 1)]
    backward = [(i + 1, i) for i in range(devices - 1)]
    low = lax.ppermute(cellhist[-RIM:], ("cell", "own"), forward)
    high = lax.ppermute(cellhist[:RIM], ("cell", "own"), backward)
    return fit(cellhist, low, high, offsets)


def solution(mesh):
    placed = (
        P(("cell", "own"), None, None),
        P(("cell", "own"), None),
        P(("cell", "own")),
        P(None, ("cell", "own")),
    )
    return jax.shard_map(
        body,
        mesh=mesh,
        in_specs=placed,
        out_specs=(P(None, None, ("cell", "own")), P(None, ("cell", "own"))),
        check_vma=False,
    )
```

```python
import functools
import jax
import jax.numpy as jnp
import numpy as np
from jax import lax
from jax.experimental import pallas as pl
from jax.experimental.pallas import tpu as pltpu
from jax.sharding import PartitionSpec as P

SPEC = 2
MOM = 6
NEWTON = 8
NEIGH = 4
W = 4
TILE = 256
RIM = 8
BF = jnp.bfloat16
F32 = jnp.float32


def legendre_rows(levels, count):
    xpos = (2.0 * np.arange(levels) + 1.0) / levels - 1.0
    table = [np.ones_like(xpos), xpos]
    for order in range(1, count - 1):
        table.append(((2 * order + 1) * xpos * table[order] - order * table[order - 1]) / (order + 1))
    return np.stack(table, axis=0)


def product_weights(count):
    weights = {}
    for m in range(1, count + 1):
        for n in range(1, m + 1):
            series = np.polynomial.legendre.legmul(np.eye(m + 1)[m], np.eye(n + 1)[n])
            weights[m, n] = [(k, float(v)) for k, v in enumerate(series) if abs(v) > 1e-12]
    return weights


def halves(value):
    high = value.astype(BF)
    return high, (value - high.astype(F32)).astype(BF)


def fit_tables(levels):
    rows = np.zeros((16, levels))
    rows[: 2 * MOM + 1] = legendre_rows(levels, 2 * MOM + 1)
    high = np.asarray(rows, jnp.bfloat16)
    low = np.asarray(rows - high.astype(np.float64), jnp.bfloat16)
    gather = np.zeros((32, 2 * levels), jnp.bfloat16)
    gather[:16, :levels] = high
    gather[:16, levels:] = high
    gather[16:, :levels] = low
    spread = np.zeros((levels, 32), jnp.bfloat16)
    spread[:, 0:MOM] = high[1 : MOM + 1].T
    spread[:, 8 : 8 + MOM] = low[1 : MOM + 1].T
    spread[:, 16 : 16 + MOM] = high[1 : MOM + 1].T
    return jnp.asarray(gather), jnp.asarray(spread)


def fit_kernel(cell_ref, low_ref, high_ref, off_ref, gather_ref, spread_ref, lam_ref, stat_ref,
               ext, target, sums, lam, mu):
    cells = cell_ref.shape[0]
    levels = gather_ref.shape[1] // 2
    tiles = cells // TILE
    span = TILE + 2 * RIM
    ext[0:RIM, :] = low_ref[...]
    ext[RIM : RIM + cells, :] = cell_ref[...]
    ext[RIM + cells :, :] = high_ref[...]
    tn = (((0,), (0,)), ((), ()))

    def moments(value):
        high, low = halves(value)
        both = jnp.dot(gather_ref[...], jnp.concatenate([high, low], axis=0), preferred_element_type=F32)
        return both[:16] + both[16:]

    def exponent(group):
        value = lam[:, group, :]
        high = value.astype(BF).astype(F32)
        stacked = jnp.concatenate([high, high, value - high, jnp.zeros_like(high)], axis=0)
        return jnp.dot(spread_ref[...], stacked.astype(BF), preferred_element_type=F32)

    place = lax.broadcasted_iota(jnp.int32, (span, TILE), 0) - lax.broadcasted_iota(jnp.int32, (span, TILE), 1) - RIM
    level = lax.broadcasted_iota(jnp.int32, (levels, TILE), 0)
    for block in range(tiles):
        cols = slice(block * TILE, (block + 1) * TILE)
        picker = (place == 0).astype(F32)
        for j in range(NEIGH):
            picker = picker + (place == off_ref[j : j + 1, cols]).astype(F32)
        picker = picker.astype(BF)
        high, low = halves(ext[block * TILE : block * TILE + span, :])
        summed = lax.dot_general(high, picker, tn, preferred_element_type=F32) + lax.dot_general(
            low, picker, tn, preferred_element_type=F32
        )
        for s in range(SPEC):
            field = summed[s * levels : (s + 1) * levels]
            below = jnp.where(level == 0, 0.0, pltpu.roll(field, 1, 0))
            above = jnp.where(level == levels - 1, 0.0, pltpu.roll(field, levels - 1, 0))
            smooth = 1.0 + (0.5 * field + 0.25 * (below + above))
            group = s * tiles + block
            target[group] = smooth
            sums[:, group, :] = moments(smooth)
    inverse = 1.0 / sums[0]
    for m in range(MOM):
        mu[m] = sums[m + 1] * inverse
    lam[...] = jnp.zeros_like(lam)
    weights = product_weights(MOM)

    def step(_, carry):
        for group in range(SPEC * tiles):
            sums[:, group, :] = moments(jnp.exp(exponent(group)))
        inverse = 1.0 / sums[0]
        mean = [None] + [sums[k] * inverse for k in range(1, 2 * MOM + 1)]
        raw = [[None] * MOM for _ in range(MOM)]
        unit = [[None] * MOM for _ in range(MOM)]
        scale = [None] * MOM
        for row in range(MOM):
            for col in range(row + 1):
                total = -mean[row + 1] * mean[col + 1]
                if row == col:
                    total = total + 0.01
                for k, v in weights[row + 1, col + 1]:
                    total = total + (v if k == 0 else v * mean[k])
                for inner in range(col):
                    total = total - raw[row][inner] * unit[col][inner]
                if row == col:
                    scale[row] = 1.0 / total
                else:
                    raw[row][col] = total
                    unit[row][col] = total * scale[col]
        forward = []
        for row in range(MOM):
            total = mean[row + 1] - mu[row]
            for inner in range(row):
                total = total - unit[row][inner] * forward[inner]
            forward.append(total)
        backward = [None] * MOM
        for row in reversed(range(MOM)):
            total = forward[row] * scale[row]
            for inner in range(row + 1, MOM):
                total = total - unit[inner][row] * backward[inner]
            backward[row] = total
            lam[row] = lam[row] - 0.5 * total
        return carry

    lax.fori_loop(0, NEWTON, step, 0)
    for s in range(SPEC):
        for block in range(tiles):
            cols = slice(block * TILE, (block + 1) * TILE)
            group = s * tiles + block
            lam_ref[:, s, cols] = lam[0:MOM, group, :]
            value = exponent(group)
            norm = jnp.log(jnp.sum(jnp.exp(value), axis=0, keepdims=True))
            field = target[group]
            total = jnp.log(jnp.sum(field, axis=0, keepdims=True))
            ratio = (jnp.log(field) - value) + (norm - total)
            stat_ref[s : s + 1, cols] = (2.0 / levels) * jnp.sum(field * ratio, axis=0, keepdims=True)


def fit(cellhist, low, high, offsets):
    cells, width = cellhist.shape
    levels = width // SPEC
    groups = SPEC * cells // TILE
    gather, spread = fit_tables(levels)
    return pl.pallas_call(
        fit_kernel,
        out_shape=(
            jax.ShapeDtypeStruct((MOM, SPEC, cells), F32),
            jax.ShapeDtypeStruct((SPEC, cells), F32),
        ),
        in_specs=[pl.BlockSpec(memory_space=pltpu.VMEM)] * 6,
        out_specs=(pl.BlockSpec(memory_space=pltpu.VMEM),) * 2,
        scratch_shapes=[
            pltpu.VMEM((cells + 2 * RIM, width), F32),
            pltpu.VMEM((groups, levels, TILE), F32),
            pltpu.VMEM((16, groups, TILE), F32),
            pltpu.VMEM((8, groups, TILE), F32),
            pltpu.VMEM((8, groups, TILE), F32),
        ],
        compiler_params=pltpu.CompilerParams(vmem_limit_bytes=32 * 1024 * 1024),
        name="fit",
    )(cellhist, low, high, offsets, gather, spread)


def route_kernel(n, own_n, hist_ref, dest_ref, cell_ref, out_ref, low_ref, high_ref,
                 packed, rel, ones, send_rows, recv_rows, send_cells, recv_cells, part_out, part_in,
                 edge_out, edge_in, row_send, row_recv, cell_send, cell_recv, part_send, part_recv,
                 edge_send, edge_recv):
    half = n // 2
    rows, width = packed.shape
    cap = ones.shape[0]
    cells = out_ref.shape[0]
    tiles = cells // TILE
    me = lax.axis_index("cell") * own_n + lax.axis_index("own")
    mine = lax.rem(me, half)
    base = me - mine
    cross = mine + (half - base)
    after, before = lax.rem(me + 1, n), lax.rem(me + n - 1, n)

    def place(index):
        return (lax.div(index, own_n), lax.rem(index, own_n))

    def row_copy(kind, source, slot, peer):
        return pltpu.make_async_remote_copy(
            src_ref=send_rows.at[kind, source], dst_ref=recv_rows.at[kind, slot],
            send_sem=row_send.at[kind, source], recv_sem=row_recv.at[kind, slot],
            device_id=place(base + peer), device_id_type=pl.DeviceIdType.MESH)

    def cell_copy(source, slot, peer):
        return pltpu.make_async_remote_copy(
            src_ref=send_cells.at[source], dst_ref=recv_cells.at[slot],
            send_sem=cell_send.at[source], recv_sem=cell_recv.at[slot],
            device_id=place(base + peer), device_id_type=pl.DeviceIdType.MESH)

    def part_copy(tile):
        return pltpu.make_async_remote_copy(
            src_ref=part_out.at[tile], dst_ref=part_in.at[tile],
            send_sem=part_send.at[tile], recv_sem=part_recv.at[tile],
            device_id=place(cross), device_id_type=pl.DeviceIdType.MESH)

    def edge_copy(side):
        return pltpu.make_async_remote_copy(
            src_ref=edge_out.at[side], dst_ref=edge_in.at[side],
            send_sem=edge_send.at[side], recv_sem=edge_recv.at[side],
            device_id=place(after if side == 0 else before), device_id_type=pl.DeviceIdType.MESH)

    barrier = pltpu.get_barrier_semaphore()

    def greet(index):
        pl.semaphore_signal(barrier, inc=1, device_id=place(index), device_id_type=pl.DeviceIdType.MESH)

    def partners(action):
        def one(step, carry):
            action(lax.rem(mine + step, half))
            return carry

        lax.fori_loop(1, half, one, 0)

    partners(lambda peer: greet(base + peer))
    greet(cross)
    greet(after)
    greet(before)

    shifted = dest_ref[...] - base
    rel[...] = jnp.where(shifted < 0, shifted + n, shifted)
    packed[...] = (
        hist_ref[0].astype(F32) + hist_ref[1].astype(F32) + hist_ref[2].astype(F32)
    ).astype(BF)
    upto = (
        lax.broadcasted_iota(jnp.int32, (TILE, TILE), 0) <= lax.broadcasted_iota(jnp.int32, (TILE, TILE), 1)
    ).astype(F32).astype(BF)
    block = lax.broadcasted_iota(jnp.int32, (n, TILE), 0)
    slot = lax.broadcasted_iota(jnp.int32, (cap, TILE), 0).astype(F32)
    seen = jnp.zeros((n, 1), F32)
    slots = jnp.zeros((2 * n, cap), F32)
    for piece in range(rows // TILE):
        cols = slice(piece * TILE, (piece + 1) * TILE)
        member = (block == rel[:, cols]).astype(F32)
        count = jnp.dot(member.astype(BF), upto, preferred_element_type=F32) + seen
        rank = jnp.sum(member * count, axis=0, keepdims=True) - 1.0
        seen = count[:, TILE - 1 :]
        hot = (slot == rank).astype(F32).astype(BF)
        ones[:, cols] = hot
        cell = cell_ref[:, cols]
        major = (cell >> 5).astype(F32)
        minor = (cell & 31).astype(F32)
        named = jnp.concatenate([member * major, member * minor], axis=0).astype(BF)
        slots = slots + lax.dot_general(named, hot, (((1,), (1,)), ((), ())), preferred_element_type=F32)
    numbers = (32.0 * slots[:n] + slots[n:]).astype(jnp.int32)
    send_cells[:, 0, :] = numbers[:half]
    send_cells[:, 1, :] = numbers[half:]

    def pack(kind, peer):
        chosen = (rel[...] == kind * half + peer).astype(F32).astype(BF)
        return jnp.dot(ones[...] * chosen, packed[...], preferred_element_type=F32).astype(BF)

    pl.semaphore_wait(barrier, half + 2)

    def first(peer):
        cell_copy(peer, mine, peer).start()
        send_rows[1, peer] = pack(1, peer)
        row_copy(1, peer, mine, peer).start()

    partners(first)
    recv_rows[1, mine] = pack(1, mine)
    recv_cells[mine] = send_cells[mine]

    def second(peer):
        send_rows[0, peer] = pack(0, peer)

    partners(second)
    recv_rows[0, mine] = pack(0, mine)

    def arrived(kind):
        def one(peer):
            if kind == 1:
                cell_copy(peer, peer, peer).wait_recv()
            row_copy(kind, peer, peer, peer).wait_recv()

        partners(one)
        return jnp.concatenate([recv_cells[s, kind : kind + 1, :] for s in range(half)], axis=1)

    def gathered(kind, names, tile):
        cell = lax.broadcasted_iota(jnp.int32, (TILE, half * cap), 0) + tile * TILE
        select = (cell == names).astype(F32).astype(BF)
        return jnp.dot(select, recv_rows[kind].reshape(half * cap, width), preferred_element_type=F32)

    order = [0, tiles - 1] + list(range(1, tiles - 1))
    names = arrived(1)
    for tile in order:
        part_out[tile] = gathered(1, names, tile).astype(BF)
        part_copy(tile).start()
    partners(lambda peer: row_copy(0, peer, mine, peer).start())
    names = arrived(0)
    for tile in order:
        out_ref[tile * TILE : (tile + 1) * TILE, :] = gathered(0, names, tile)
    for at, tile in enumerate(order):
        part_copy(tile).wait_recv()
        span = slice(tile * TILE, (tile + 1) * TILE)
        out_ref[span, :] = out_ref[span, :] + part_in[tile].astype(F32)
        if at == 1:
            edge_out[0] = out_ref[cells - RIM :, :]
            edge_out[1] = out_ref[:RIM, :]
            edge_copy(0).start()
            edge_copy(1).start()
    edge_copy(0).wait_recv()
    edge_copy(1).wait_recv()
    low_ref[...] = jnp.where(me == 0, 0.0, edge_in[0])
    high_ref[...] = jnp.where(me == n - 1, 0.0, edge_in[1])

    def sent(peer):
        cell_copy(peer, mine, peer).wait_send()
        row_copy(0, peer, mine, peer).wait_send()
        row_copy(1, peer, mine, peer).wait_send()

    partners(sent)
    for tile in order:
        part_copy(tile).wait_send()
    edge_copy(0).wait_send()
    edge_copy(1).wait_send()


def route(hist, dest, cell_in, cells):
    replicas, rows, width = hist.shape
    n, own_n = lax.axis_size(("cell", "own")), lax.axis_size("own")
    half, cap, tiles = n // 2, 2 * rows // n, cells // TILE
    dma = pltpu.SemaphoreType.DMA
    return pl.pallas_call(
        functools.partial(route_kernel, n, own_n),
        out_shape=(
            jax.ShapeDtypeStruct((cells, width), F32),
            jax.ShapeDtypeStruct((RIM, width), F32),
            jax.ShapeDtypeStruct((RIM, width), F32),
        ),
        in_specs=[pl.BlockSpec(memory_space=pltpu.VMEM)] * 3,
        out_specs=(pl.BlockSpec(memory_space=pltpu.VMEM),) * 3,
        scratch_shapes=[
            pltpu.VMEM((rows, width), BF),
            pltpu.VMEM((1, rows), jnp.int32),
            pltpu.VMEM((cap, rows), BF),
            pltpu.VMEM((2, half, cap, width), BF),
            pltpu.VMEM((2, half, cap, width), BF),
            pltpu.VMEM((half, 2, cap), jnp.int32),
            pltpu.VMEM((half, 2, cap), jnp.int32),
            pltpu.VMEM((tiles, TILE, width), BF),
            pltpu.VMEM((tiles, TILE, width), BF),
            pltpu.VMEM((2, RIM, width), F32),
            pltpu.VMEM((2, RIM, width), F32),
            dma((2, half)),
            dma((2, half)),
            dma((half,)),
            dma((half,)),
            dma((tiles,)),
            dma((tiles,)),
            dma((2,)),
            dma((2,)),
        ],
        compiler_params=pltpu.CompilerParams(
            collective_id=0, has_side_effects=True, vmem_limit_bytes=40 * 1024 * 1024
        ),
        name="route",
    )(hist, dest, cell_in)


def body(hist, dest, cell_in, offsets):
    rows = hist.shape[0]
    cellhist, low, high = route(
        jnp.transpose(hist, (1, 0, 2)), dest.reshape(1, rows), cell_in.reshape(1, rows), offsets.shape[1]
    )
    lam, stat = fit(cellhist, low, high, offsets)
    return jnp.transpose(lam, (1, 0, 2)), stat


def solution(mesh):
    placed = (
        P(("cell", "own"), None, None),
        P(("cell", "own"), None),
        P(("cell", "own")),
        P(None, ("cell", "own")),
    )
    return jax.shard_map(
        body,
        mesh=mesh,
        in_specs=placed,
        out_specs=(P(None, None, ("cell", "own")), P(None, ("cell", "own"))),
        check_vma=False,
    )
```

```python
import functools
import jax
import jax.numpy as jnp
import numpy as np
from jax import lax
from jax.experimental import pallas as pl
from jax.experimental.pallas import tpu as pltpu
from jax.sharding import PartitionSpec as P

SPEC = 2
MOM = 6
NEWTON = 8
NEIGH = 4
W = 4
TILE = 256
RIM = 8
BF = jnp.bfloat16
F32 = jnp.float32


def legendre_rows(levels, count):
    xpos = (2.0 * np.arange(levels) + 1.0) / levels - 1.0
    table = [np.ones_like(xpos), xpos]
    for order in range(1, count - 1):
        table.append(((2 * order + 1) * xpos * table[order] - order * table[order - 1]) / (order + 1))
    return np.stack(table, axis=0)


def product_weights(count):
    weights = {}
    for m in range(1, count + 1):
        for n in range(1, m + 1):
            series = np.polynomial.legendre.legmul(np.eye(m + 1)[m], np.eye(n + 1)[n])
            weights[m, n] = [(k, float(v)) for k, v in enumerate(series) if abs(v) > 1e-12]
    return weights


def halves(value):
    high = value.astype(BF)
    return high, (value - high.astype(F32)).astype(BF)


def fit_tables(levels):
    rows = np.zeros((16, levels))
    rows[: 2 * MOM + 1] = legendre_rows(levels, 2 * MOM + 1)
    high = np.asarray(rows, jnp.bfloat16)
    low = np.asarray(rows - high.astype(np.float64), jnp.bfloat16)
    gather = np.zeros((32, 2 * levels), jnp.bfloat16)
    gather[:16, :levels] = high
    gather[:16, levels:] = high
    gather[16:, :levels] = low
    spread = np.zeros((levels, 32), jnp.bfloat16)
    spread[:, 0:MOM] = high[1 : MOM + 1].T
    spread[:, 8 : 8 + MOM] = low[1 : MOM + 1].T
    spread[:, 16 : 16 + MOM] = high[1 : MOM + 1].T
    return jnp.asarray(gather), jnp.asarray(spread)


def fit_kernel(cell_ref, low_ref, high_ref, off_ref, gather_ref, spread_ref, lam_ref, stat_ref,
               ext, target, sums, lam, mu):
    cells = cell_ref.shape[0]
    levels = gather_ref.shape[1] // 2
    tiles = cells // TILE
    span = TILE + 2 * RIM
    ext[0:RIM, :] = low_ref[...]
    ext[RIM : RIM + cells, :] = cell_ref[...]
    ext[RIM + cells :, :] = high_ref[...]
    tn = (((0,), (0,)), ((), ()))

    def moments(value):
        high, low = halves(value)
        both = jnp.dot(gather_ref[...], jnp.concatenate([high, low], axis=0), preferred_element_type=F32)
        return both[:16] + both[16:]

    def exponent(group):
        value = lam[:, group, :]
        high = value.astype(BF).astype(F32)
        stacked = jnp.concatenate([high, high, value - high, jnp.zeros_like(high)], axis=0)
        return jnp.dot(spread_ref[...], stacked.astype(BF), preferred_element_type=F32)

    place = lax.broadcasted_iota(jnp.int32, (span, TILE), 0) - lax.broadcasted_iota(jnp.int32, (span, TILE), 1) - RIM
    level = lax.broadcasted_iota(jnp.int32, (levels, TILE), 0)
    for block in range(tiles):
        cols = slice(block * TILE, (block + 1) * TILE)
        picker = (place == 0).astype(F32)
        for j in range(NEIGH):
            picker = picker + (place == off_ref[j : j + 1, cols]).astype(F32)
        picker = picker.astype(BF)
        high, low = halves(ext[block * TILE : block * TILE + span, :])
        summed = lax.dot_general(high, picker, tn, preferred_element_type=F32) + lax.dot_general(
            low, picker, tn, preferred_element_type=F32
        )
        for s in range(SPEC):
            field = summed[s * levels : (s + 1) * levels]
            below = jnp.where(level == 0, 0.0, pltpu.roll(field, 1, 0))
            above = jnp.where(level == levels - 1, 0.0, pltpu.roll(field, levels - 1, 0))
            smooth = 1.0 + (0.5 * field + 0.25 * (below + above))
            group = s * tiles + block
            target[group] = smooth
            sums[:, group, :] = moments(smooth)
    inverse = 1.0 / sums[0]
    for m in range(MOM):
        mu[m] = sums[m + 1] * inverse
    weights = product_weights(MOM)
    flat = legendre_rows(levels, 2 * MOM + 1).mean(axis=1)
    hess = np.array([
        [sum(v * flat[k] for k, v in weights[max(m, n), min(m, n)]) - flat[m] * flat[n] + 0.01 * (m == n)
         for n in range(1, MOM + 1)]
        for m in range(1, MOM + 1)
    ])
    solved = 0.5 * np.linalg.inv(hess)
    for m in range(MOM):
        total = jnp.zeros_like(mu[0])
        for k in range(MOM):
            if abs(solved[m, k]) > 1e-14:
                total = total + float(solved[m, k]) * (mu[k] - float(flat[k + 1]))
        lam[m] = total
    for m in range(MOM, 8):
        lam[m] = jnp.zeros_like(mu[0])

    def step(_, carry):
        for group in range(SPEC * tiles):
            sums[:, group, :] = moments(jnp.exp(exponent(group)))
        inverse = 1.0 / sums[0]
        mean = [None] + [sums[k] * inverse for k in range(1, 2 * MOM + 1)]
        raw = [[None] * MOM for _ in range(MOM)]
        unit = [[None] * MOM for _ in range(MOM)]
        scale = [None] * MOM
        for row in range(MOM):
            for col in range(row + 1):
                total = -mean[row + 1] * mean[col + 1]
                if row == col:
                    total = total + 0.01
                for k, v in weights[row + 1, col + 1]:
                    total = total + (v if k == 0 else v * mean[k])
                for inner in range(col):
                    total = total - raw[row][inner] * unit[col][inner]
                if row == col:
                    scale[row] = 1.0 / total
                else:
                    raw[row][col] = total
                    unit[row][col] = total * scale[col]
        forward = []
        for row in range(MOM):
            total = mean[row + 1] - mu[row]
            for inner in range(row):
                total = total - unit[row][inner] * forward[inner]
            forward.append(total)
        backward = [None] * MOM
        for row in reversed(range(MOM)):
            total = forward[row] * scale[row]
            for inner in range(row + 1, MOM):
                total = total - unit[inner][row] * backward[inner]
            backward[row] = total
            lam[row] = lam[row] - 0.5 * total
        return carry

    lax.fori_loop(1, NEWTON, step, 0)
    for s in range(SPEC):
        for block in range(tiles):
            cols = slice(block * TILE, (block + 1) * TILE)
            group = s * tiles + block
            lam_ref[:, s, cols] = lam[0:MOM, group, :]
            value = exponent(group)
            norm = jnp.log(jnp.sum(jnp.exp(value), axis=0, keepdims=True))
            field = target[group]
            total = jnp.log(jnp.sum(field, axis=0, keepdims=True))
            ratio = (jnp.log(field) - value) + (norm - total)
            stat_ref[s : s + 1, cols] = (2.0 / levels) * jnp.sum(field * ratio, axis=0, keepdims=True)


def fit(cellhist, low, high, offsets):
    cells, width = cellhist.shape
    levels = width // SPEC
    groups = SPEC * cells // TILE
    gather, spread = fit_tables(levels)
    return pl.pallas_call(
        fit_kernel,
        out_shape=(
            jax.ShapeDtypeStruct((MOM, SPEC, cells), F32),
            jax.ShapeDtypeStruct((SPEC, cells), F32),
        ),
        in_specs=[pl.BlockSpec(memory_space=pltpu.VMEM)] * 6,
        out_specs=(pl.BlockSpec(memory_space=pltpu.VMEM),) * 2,
        scratch_shapes=[
            pltpu.VMEM((cells + 2 * RIM, width), F32),
            pltpu.VMEM((groups, levels, TILE), F32),
            pltpu.VMEM((16, groups, TILE), F32),
            pltpu.VMEM((8, groups, TILE), F32),
            pltpu.VMEM((8, groups, TILE), F32),
        ],
        compiler_params=pltpu.CompilerParams(vmem_limit_bytes=32 * 1024 * 1024),
        name="fit",
    )(cellhist, low, high, offsets, gather, spread)


def route_kernel(n, own_n, hist_hbm, dest_hbm, cell_hbm, out_ref, low_ref, high_ref,
                 hist, dest, cell_in, packed, rel, ones, near_out, near_in, far_out, far_in,
                 send_cells, recv_cells, part_out, part_in, edge_out, edge_in,
                 load, near_send, near_recv, far_send, far_recv, cell_send, cell_recv,
                 part_send, part_recv, edge_send, edge_recv):
    half = n // 2
    rows, width = packed.shape
    levels = width // SPEC
    cap = ones.shape[0]
    cells = out_ref.shape[0]
    tiles = cells // TILE
    me = lax.axis_index("cell") * own_n + lax.axis_index("own")
    after, before = lax.rem(me + 1, n), lax.rem(me + n - 1, n)
    bits = [lax.rem(lax.div(me, 1 << b), 2) for b in range(n.bit_length() - 1)]

    def flipped(mask):
        index = me
        for b, bit in enumerate(bits):
            if mask >> b & 1:
                index = index + (1 << b) * (1 - 2 * bit)
        return index

    def place(index):
        return (lax.div(index, own_n), lax.rem(index, own_n))

    def remote(source, target, sent, received, index):
        return pltpu.make_async_remote_copy(
            src_ref=source, dst_ref=target, send_sem=sent, recv_sem=received,
            device_id=place(index), device_id_type=pl.DeviceIdType.MESH)

    def near_copy(mask):
        return remote(near_out.at[mask], near_in.at[mask], near_send.at[mask], near_recv.at[mask], flipped(mask))

    def far_copy(s, mask):
        return remote(far_out.at[s, mask], far_in.at[s, mask], far_send.at[s, mask], far_recv.at[s, mask], flipped(mask))

    def cell_copy(mask):
        return remote(send_cells.at[mask], recv_cells.at[mask], cell_send.at[mask], cell_recv.at[mask], flipped(mask))

    def part_copy(s, tile):
        return remote(part_out.at[s, tile], part_in.at[s, tile], part_send.at[s, tile], part_recv.at[s, tile], flipped(half))

    def edge_copy(side):
        return remote(edge_out.at[side], edge_in.at[side], edge_send.at[side], edge_recv.at[side],
                      after if side == 0 else before)

    loads = [
        pltpu.make_async_copy(dest_hbm, dest, load.at[0]),
        pltpu.make_async_copy(cell_hbm, cell_in, load.at[1]),
        pltpu.make_async_copy(hist_hbm, hist, load.at[2]),
    ]
    for copy in loads:
        copy.start()

    barrier = pltpu.get_barrier_semaphore()
    for index in [flipped(mask) for mask in range(1, half + 1)] + [after, before]:
        pl.semaphore_signal(barrier, inc=1, device_id=place(index), device_id_type=pl.DeviceIdType.MESH)

    loads[0].wait()
    rel[...] = dest[...] ^ me
    loads[1].wait()
    upto = (
        lax.broadcasted_iota(jnp.int32, (TILE, TILE), 0) <= lax.broadcasted_iota(jnp.int32, (TILE, TILE), 1)
    ).astype(F32).astype(BF)
    block = lax.broadcasted_iota(jnp.int32, (n, TILE), 0)
    slot = lax.broadcasted_iota(jnp.int32, (cap, TILE), 0).astype(F32)
    seen = jnp.zeros((n, 1), F32)
    slots = jnp.zeros((2 * n, cap), F32)
    for piece in range(rows // TILE):
        cols = slice(piece * TILE, (piece + 1) * TILE)
        member = (block == rel[:, cols]).astype(F32)
        count = jnp.dot(member.astype(BF), upto, preferred_element_type=F32) + seen
        rank = jnp.sum(member * count, axis=0, keepdims=True) - 1.0
        seen = count[:, TILE - 1 :]
        hot = (slot == rank).astype(F32).astype(BF)
        ones[:, cols] = hot
        cell = cell_in[:, cols]
        major = (cell >> 5).astype(F32)
        minor = (cell & 31).astype(F32)
        named = jnp.concatenate([member * major, member * minor], axis=0).astype(BF)
        slots = slots + lax.dot_general(named, hot, (((1,), (1,)), ((), ())), preferred_element_type=F32)
    numbers = (32.0 * slots[:n] + slots[n:]).astype(jnp.int32)
    send_cells[:, 0, :] = numbers[:half]
    send_cells[:, 1, :] = numbers[half:]
    loads[2].wait()
    packed[...] = (hist[0].astype(F32) + hist[1].astype(F32) + hist[2].astype(F32)).astype(BF)

    def pack(kind, masks):
        chosen = [(rel[...] == kind * half + mask).astype(F32).astype(BF) for mask in masks]
        picked = jnp.concatenate([ones[...] * row for row in chosen], axis=0)
        return jnp.dot(picked, packed[...], preferred_element_type=F32).astype(BF)

    stride = half // 4
    groups = [[q + j * stride for j in range(4)] for q in sorted(range(stride), key=lambda q: (q % 2, -q))]

    pl.semaphore_wait(barrier, half + 2)
    for mask in range(1, half):
        cell_copy(mask).start()
    for masks in groups:
        value = pack(1, masks)
        for j, mask in enumerate(masks):
            for s in range(SPEC):
                piece = value[j * cap : (j + 1) * cap, s * levels : (s + 1) * levels]
                if mask == 0:
                    far_in[s, mask] = piece
                else:
                    far_out[s, mask] = piece
            if mask != 0:
                far_copy(0, mask).start()
    for masks in groups:
        for mask in masks:
            if mask != 0:
                far_copy(1, mask).start()
    recv_cells[0] = send_cells[0]
    for masks in groups:
        value = pack(0, masks)
        for j, mask in enumerate(masks):
            piece = value[j * cap : (j + 1) * cap]
            if mask == 0:
                near_in[mask] = piece
            else:
                near_out[mask] = piece

    for mask in range(1, half):
        cell_copy(mask).wait_recv()

    def names(kind):
        return jnp.concatenate([recv_cells[mask, kind : kind + 1, :] for mask in range(half)], axis=1)

    def gathered(name, pair, value):
        cell = lax.broadcasted_iota(jnp.int32, (TILE, half * cap), 0)
        select = jnp.concatenate(
            [(cell == name - tile * TILE).astype(F32).astype(BF) for tile in pair], axis=0
        )
        return jnp.dot(select, value, preferred_element_type=F32)

    order = [0, tiles - 1] + list(range(1, tiles - 1))
    pairs = [order[i : i + 2] for i in range(0, tiles, 2)]
    name = names(1)
    for s in range(SPEC):
        for mask in range(1, half):
            far_copy(s, mask).wait_recv()
        for pair in pairs:
            value = gathered(name, pair, far_in[s].reshape(half * cap, levels)).astype(BF)
            for j, tile in enumerate(pair):
                part_out[s, tile] = value[j * TILE : (j + 1) * TILE]
                part_copy(s, tile).start()
    for masks in groups:
        for mask in masks:
            if mask != 0:
                near_copy(mask).start()
    for mask in range(1, half):
        near_copy(mask).wait_recv()
    name = names(0)
    for pair in pairs:
        value = gathered(name, pair, near_in[...].reshape(half * cap, width))
        for j, tile in enumerate(pair):
            out_ref[tile * TILE : (tile + 1) * TILE, :] = value[j * TILE : (j + 1) * TILE]
    for s in range(SPEC):
        lanes = slice(s * levels, (s + 1) * levels)
        for pair in pairs:
            for tile in pair:
                part_copy(s, tile).wait_recv()
                span = slice(tile * TILE, (tile + 1) * TILE)
                out_ref[span, lanes] = out_ref[span, lanes] + part_in[s, tile].astype(F32)
            if s == SPEC - 1 and pair is pairs[0]:
                edge_out[0] = out_ref[cells - RIM :, :]
                edge_out[1] = out_ref[:RIM, :]
                edge_copy(0).start()
                edge_copy(1).start()
    edge_copy(0).wait_recv()
    edge_copy(1).wait_recv()
    low_ref[...] = jnp.where(me == 0, 0.0, edge_in[0])
    high_ref[...] = jnp.where(me == n - 1, 0.0, edge_in[1])

    for mask in range(1, half):
        cell_copy(mask).wait_send()
        near_copy(mask).wait_send()
        for s in range(SPEC):
            far_copy(s, mask).wait_send()
    for tile in order:
        for s in range(SPEC):
            part_copy(s, tile).wait_send()
    edge_copy(0).wait_send()
    edge_copy(1).wait_send()


def route(hist, dest, cell_in, cells):
    replicas, rows, width = hist.shape
    n, own_n = lax.axis_size(("cell", "own")), lax.axis_size("own")
    half, cap, tiles, levels = n // 2, 2 * rows // n, cells // TILE, width // SPEC
    dma = pltpu.SemaphoreType.DMA
    return pl.pallas_call(
        functools.partial(route_kernel, n, own_n),
        out_shape=(
            jax.ShapeDtypeStruct((cells, width), F32),
            jax.ShapeDtypeStruct((RIM, width), F32),
            jax.ShapeDtypeStruct((RIM, width), F32),
        ),
        in_specs=[pl.BlockSpec(memory_space=pl.ANY)] * 3,
        out_specs=(pl.BlockSpec(memory_space=pltpu.VMEM),) * 3,
        scratch_shapes=[
            pltpu.VMEM((replicas, rows, width), BF),
            pltpu.VMEM((1, rows), jnp.int32),
            pltpu.VMEM((1, rows), jnp.int32),
            pltpu.VMEM((rows, width), BF),
            pltpu.VMEM((1, rows), jnp.int32),
            pltpu.VMEM((cap, rows), BF),
            pltpu.VMEM((half, cap, width), BF),
            pltpu.VMEM((half, cap, width), BF),
            pltpu.VMEM((SPEC, half, cap, levels), BF),
            pltpu.VMEM((SPEC, half, cap, levels), BF),
            pltpu.VMEM((half, 2, cap), jnp.int32),
            pltpu.VMEM((half, 2, cap), jnp.int32),
            pltpu.VMEM((SPEC, tiles, TILE, levels), BF),
            pltpu.VMEM((SPEC, tiles, TILE, levels), BF),
            pltpu.VMEM((2, RIM, width), F32),
            pltpu.VMEM((2, RIM, width), F32),
            dma((3,)),
            dma((half,)),
            dma((half,)),
            dma((SPEC, half)),
            dma((SPEC, half)),
            dma((half,)),
            dma((half,)),
            dma((SPEC, tiles)),
            dma((SPEC, tiles)),
            dma((2,)),
            dma((2,)),
        ],
        compiler_params=pltpu.CompilerParams(
            collective_id=0, has_side_effects=True, vmem_limit_bytes=48 * 1024 * 1024
        ),
        name="route",
    )(hist, dest, cell_in)


def body(hist, dest, cell_in, offsets):
    rows = hist.shape[0]
    cellhist, low, high = route(
        jnp.transpose(hist, (1, 0, 2)), dest.reshape(1, rows), cell_in.reshape(1, rows), offsets.shape[1]
    )
    lam, stat = fit(cellhist, low, high, offsets)
    return jnp.transpose(lam, (1, 0, 2)), stat


def solution(mesh):
    placed = (
        P(("cell", "own"), None, None),
        P(("cell", "own"), None),
        P(("cell", "own")),
        P(None, ("cell", "own")),
    )
    return jax.shard_map(
        body,
        mesh=mesh,
        in_specs=placed,
        out_specs=(P(None, None, ("cell", "own")), P(None, ("cell", "own"))),
        check_vma=False,
    )
```

```python
import functools
import jax
import jax.numpy as jnp
import numpy as np
from jax import lax
from jax.experimental import pallas as pl
from jax.experimental.pallas import tpu as pltpu
from jax.sharding import PartitionSpec as P

SPEC = 2
MOM = 6
NEWTON = 8
NEIGH = 4
W = 4
TILE = 256
RIM = 8
BF = jnp.bfloat16
F32 = jnp.float32


def legendre_rows(levels, count):
    xpos = (2.0 * np.arange(levels) + 1.0) / levels - 1.0
    table = [np.ones_like(xpos), xpos]
    for order in range(1, count - 1):
        table.append(((2 * order + 1) * xpos * table[order] - order * table[order - 1]) / (order + 1))
    return np.stack(table, axis=0)


def product_weights(count):
    weights = {}
    for m in range(1, count + 1):
        for n in range(1, m + 1):
            series = np.polynomial.legendre.legmul(np.eye(m + 1)[m], np.eye(n + 1)[n])
            weights[m, n] = [(k, float(v)) for k, v in enumerate(series) if abs(v) > 1e-12]
    return weights


def halves(value):
    high = value.astype(BF)
    return high, (value - high.astype(F32)).astype(BF)


def fit_tables(levels):
    rows = np.zeros((16, levels))
    rows[: 2 * MOM + 1] = legendre_rows(levels, 2 * MOM + 1)
    high = np.asarray(rows, jnp.bfloat16)
    low = np.asarray(rows - high.astype(np.float64), jnp.bfloat16)
    gather = np.zeros((32, 2 * levels), jnp.bfloat16)
    gather[:16, :levels] = high
    gather[:16, levels:] = high
    gather[16:, :levels] = low
    spread = np.zeros((levels, 32), jnp.bfloat16)
    spread[:, 0:MOM] = high[1 : MOM + 1].T
    spread[:, 8 : 8 + MOM] = low[1 : MOM + 1].T
    spread[:, 16 : 16 + MOM] = high[1 : MOM + 1].T
    return jnp.asarray(gather), jnp.asarray(spread)


def fit_kernel(cell_ref, low_ref, high_ref, off_ref, gather_ref, spread_ref, lam_ref, stat_ref,
               ext, target, sums, lam, mu):
    cells = cell_ref.shape[0]
    levels = gather_ref.shape[1] // 2
    tiles = cells // TILE
    span = TILE + 2 * RIM
    ext[0:RIM, :] = low_ref[...]
    ext[RIM : RIM + cells, :] = cell_ref[...]
    ext[RIM + cells :, :] = high_ref[...]
    tn = (((0,), (0,)), ((), ()))

    def moments(value):
        high, low = halves(value)
        both = jnp.dot(gather_ref[...], jnp.concatenate([high, low], axis=0), preferred_element_type=F32)
        return both[:16] + both[16:]

    def exponent(group):
        value = lam[group // tiles, :, group % tiles, :]
        high = value.astype(BF).astype(F32)
        stacked = jnp.concatenate([high, high, value - high, jnp.zeros_like(high)], axis=0)
        return jnp.dot(spread_ref[...], stacked.astype(BF), preferred_element_type=F32)

    place = lax.broadcasted_iota(jnp.int32, (span, TILE), 0) - lax.broadcasted_iota(jnp.int32, (span, TILE), 1) - RIM
    level = lax.broadcasted_iota(jnp.int32, (levels, TILE), 0)
    for block in range(tiles):
        cols = slice(block * TILE, (block + 1) * TILE)
        picker = (place == 0).astype(F32)
        for j in range(NEIGH):
            picker = picker + (place == off_ref[j : j + 1, cols]).astype(F32)
        picker = picker.astype(BF)
        high, low = halves(ext[block * TILE : block * TILE + span, :])
        summed = lax.dot_general(high, picker, tn, preferred_element_type=F32) + lax.dot_general(
            low, picker, tn, preferred_element_type=F32
        )
        for s in range(SPEC):
            field = summed[s * levels : (s + 1) * levels]
            below = jnp.where(level == 0, 0.0, pltpu.roll(field, 1, 0))
            above = jnp.where(level == levels - 1, 0.0, pltpu.roll(field, levels - 1, 0))
            smooth = 1.0 + (0.5 * field + 0.25 * (below + above))
            group = s * tiles + block
            target[group] = smooth
            sums[s, :, block, :] = moments(smooth)
    weights = product_weights(MOM)
    flat = legendre_rows(levels, 2 * MOM + 1).mean(axis=1)
    hess = np.array([
        [sum(v * flat[k] for k, v in weights[max(m, n), min(m, n)]) - flat[m] * flat[n] + 0.01 * (m == n)
         for n in range(1, MOM + 1)]
        for m in range(1, MOM + 1)
    ])
    solved = 0.5 * np.linalg.inv(hess)
    for s in range(SPEC):
        inverse = 1.0 / sums[s, 0]
        for m in range(MOM):
            mu[s, m] = sums[s, m + 1] * inverse
        for m in range(MOM):
            total = jnp.zeros_like(inverse)
            for k in range(MOM):
                if abs(solved[m, k]) > 1e-14:
                    total = total + float(solved[m, k]) * (mu[s, k] - float(flat[k + 1]))
            lam[s, m] = total
        for m in range(MOM, 8):
            lam[s, m] = jnp.zeros_like(inverse)

    def measure(s):
        for block in range(tiles):
            sums[s, :, block, :] = moments(jnp.exp(exponent(s * tiles + block)))

    def update(s):
        inverse = 1.0 / sums[s, 0]
        mean = [None] + [sums[s, k] * inverse for k in range(1, 2 * MOM + 1)]
        raw = [[None] * MOM for _ in range(MOM)]
        unit = [[None] * MOM for _ in range(MOM)]
        scale = [None] * MOM
        for row in range(MOM):
            for col in range(row + 1):
                total = -mean[row + 1] * mean[col + 1]
                if row == col:
                    total = total + 0.01
                for k, v in weights[row + 1, col + 1]:
                    total = total + (v if k == 0 else v * mean[k])
                for inner in range(col):
                    total = total - raw[row][inner] * unit[col][inner]
                if row == col:
                    scale[row] = 1.0 / total
                else:
                    raw[row][col] = total
                    unit[row][col] = total * scale[col]
        forward = []
        for row in range(MOM):
            total = mean[row + 1] - mu[s, row]
            for inner in range(row):
                total = total - unit[row][inner] * forward[inner]
            forward.append(total)
        backward = [None] * MOM
        for row in reversed(range(MOM)):
            total = forward[row] * scale[row]
            for inner in range(row + 1, MOM):
                total = total - unit[inner][row] * backward[inner]
            backward[row] = total
            lam[s, row] = lam[s, row] - 0.5 * total

    measure(0)

    def step(_, carry):
        measure(1)
        update(0)
        measure(0)
        update(1)
        return carry

    lax.fori_loop(1, NEWTON, step, 0)
    for s in range(SPEC):
        for block in range(tiles):
            cols = slice(block * TILE, (block + 1) * TILE)
            group = s * tiles + block
            lam_ref[:, s, cols] = lam[s, 0:MOM, block, :]
            value = exponent(group)
            norm = jnp.log(jnp.sum(jnp.exp(value), axis=0, keepdims=True))
            field = target[group]
            total = jnp.log(jnp.sum(field, axis=0, keepdims=True))
            ratio = (jnp.log(field) - value) + (norm - total)
            stat_ref[s : s + 1, cols] = (2.0 / levels) * jnp.sum(field * ratio, axis=0, keepdims=True)


def fit(cellhist, low, high, offsets):
    cells, width = cellhist.shape
    levels = width // SPEC
    groups = SPEC * cells // TILE
    gather, spread = fit_tables(levels)
    return pl.pallas_call(
        fit_kernel,
        out_shape=(
            jax.ShapeDtypeStruct((MOM, SPEC, cells), F32),
            jax.ShapeDtypeStruct((SPEC, cells), F32),
        ),
        in_specs=[pl.BlockSpec(memory_space=pltpu.VMEM)] * 6,
        out_specs=(pl.BlockSpec(memory_space=pltpu.VMEM),) * 2,
        scratch_shapes=[
            pltpu.VMEM((cells + 2 * RIM, width), F32),
            pltpu.VMEM((groups, levels, TILE), F32),
            pltpu.VMEM((SPEC, 16, groups // SPEC, TILE), F32),
            pltpu.VMEM((SPEC, 8, groups // SPEC, TILE), F32),
            pltpu.VMEM((SPEC, 8, groups // SPEC, TILE), F32),
        ],
        compiler_params=pltpu.CompilerParams(vmem_limit_bytes=32 * 1024 * 1024),
        name="fit",
    )(cellhist, low, high, offsets, gather, spread)


def route_kernel(n, own_n, hist_hbm, dest_hbm, cell_hbm, out_ref, low_ref, high_ref,
                 hist, dest, cell_in, packed, rel, ones, near_out, near_in, far_out, far_in,
                 send_cells, recv_cells, part_out, part_in, edge_out, edge_in,
                 load, near_send, near_recv, far_send, far_recv, cell_send, cell_recv,
                 part_send, part_recv, edge_send, edge_recv):
    half = n // 2
    rows, width = packed.shape
    levels = width // SPEC
    cap = ones.shape[0]
    cells = out_ref.shape[0]
    tiles = cells // TILE
    me = lax.axis_index("cell") * own_n + lax.axis_index("own")
    after, before = lax.rem(me + 1, n), lax.rem(me + n - 1, n)
    bits = [lax.rem(lax.div(me, 1 << b), 2) for b in range(n.bit_length() - 1)]

    def flipped(mask):
        index = me
        for b, bit in enumerate(bits):
            if mask >> b & 1:
                index = index + (1 << b) * (1 - 2 * bit)
        return index

    def place(index):
        return (lax.div(index, own_n), lax.rem(index, own_n))

    def remote(source, target, sent, received, index):
        return pltpu.make_async_remote_copy(
            src_ref=source, dst_ref=target, send_sem=sent, recv_sem=received,
            device_id=place(index), device_id_type=pl.DeviceIdType.MESH)

    def near_copy(mask):
        return remote(near_out.at[mask], near_in.at[mask], near_send.at[mask], near_recv.at[mask], flipped(mask))

    def far_copy(s, mask):
        return remote(far_out.at[s, mask], far_in.at[s, mask], far_send.at[s, mask], far_recv.at[s, mask], flipped(mask))

    def cell_copy(mask):
        return remote(send_cells.at[mask], recv_cells.at[mask], cell_send.at[mask], cell_recv.at[mask], flipped(mask))

    def part_copy(s, tile):
        return remote(part_out.at[s, tile], part_in.at[s, tile], part_send.at[s, tile], part_recv.at[s, tile], flipped(half))

    def edge_copy(side):
        return remote(edge_out.at[side], edge_in.at[side], edge_send.at[side], edge_recv.at[side],
                      after if side == 0 else before)

    loads = [
        pltpu.make_async_copy(dest_hbm, dest, load.at[0]),
        pltpu.make_async_copy(cell_hbm, cell_in, load.at[1]),
        pltpu.make_async_copy(hist_hbm, hist, load.at[2]),
    ]
    for copy in loads:
        copy.start()

    barrier = pltpu.get_barrier_semaphore()
    for index in [flipped(mask) for mask in range(1, half + 1)] + [after, before]:
        pl.semaphore_signal(barrier, inc=1, device_id=place(index), device_id_type=pl.DeviceIdType.MESH)

    loads[0].wait()
    rel[...] = dest[...] ^ me
    loads[1].wait()
    upto = (
        lax.broadcasted_iota(jnp.int32, (TILE, TILE), 0) <= lax.broadcasted_iota(jnp.int32, (TILE, TILE), 1)
    ).astype(F32).astype(BF)
    block = lax.broadcasted_iota(jnp.int32, (n, TILE), 0)
    slot = lax.broadcasted_iota(jnp.int32, (cap, TILE), 0).astype(F32)
    seen = jnp.zeros((n, 1), F32)
    slots = jnp.zeros((2 * n, cap), F32)
    for piece in range(rows // TILE):
        cols = slice(piece * TILE, (piece + 1) * TILE)
        member = (block == rel[:, cols]).astype(F32)
        count = jnp.dot(member.astype(BF), upto, preferred_element_type=F32) + seen
        rank = jnp.sum(member * count, axis=0, keepdims=True) - 1.0
        seen = count[:, TILE - 1 :]
        hot = (slot == rank).astype(F32).astype(BF)
        ones[:, cols] = hot
        cell = cell_in[:, cols]
        major = (cell >> 5).astype(F32)
        minor = (cell & 31).astype(F32)
        named = jnp.concatenate([member * major, member * minor], axis=0).astype(BF)
        slots = slots + lax.dot_general(named, hot, (((1,), (1,)), ((), ())), preferred_element_type=F32)
    numbers = (32.0 * slots[:n] + slots[n:]).astype(jnp.int32)
    send_cells[:, 0, :] = numbers[:half]
    send_cells[:, 1, :] = numbers[half:]
    loads[2].wait()
    packed[...] = (hist[0].astype(F32) + hist[1].astype(F32) + hist[2].astype(F32)).astype(BF)

    def pack(kind, masks):
        chosen = [(rel[...] == kind * half + mask).astype(F32).astype(BF) for mask in masks]
        picked = jnp.concatenate([ones[...] * row for row in chosen], axis=0)
        return jnp.dot(picked, packed[...], preferred_element_type=F32).astype(BF)

    stride = half // 4
    groups = [[q + j * stride for j in range(4)] for q in sorted(range(stride), key=lambda q: (q % 2, -q))]

    pl.semaphore_wait(barrier, half + 2)
    for mask in range(1, half):
        cell_copy(mask).start()
    for masks in groups:
        value = pack(1, masks)
        for j, mask in enumerate(masks):
            for s in range(SPEC):
                piece = value[j * cap : (j + 1) * cap, s * levels : (s + 1) * levels]
                if mask == 0:
                    far_in[s, mask] = piece
                else:
                    far_out[s, mask] = piece
            if mask != 0:
                far_copy(0, mask).start()
    for masks in groups:
        for mask in masks:
            if mask != 0:
                far_copy(1, mask).start()
    recv_cells[0] = send_cells[0]
    for masks in groups:
        value = pack(0, masks)
        for j, mask in enumerate(masks):
            piece = value[j * cap : (j + 1) * cap]
            if mask == 0:
                near_in[mask] = piece
            else:
                near_out[mask] = piece

    for mask in range(1, half):
        cell_copy(mask).wait_recv()

    def names(kind):
        return jnp.concatenate([recv_cells[mask, kind : kind + 1, :] for mask in range(half)], axis=1)

    def gathered(name, pair, value):
        cell = lax.broadcasted_iota(jnp.int32, (TILE, half * cap), 0)
        select = jnp.concatenate(
            [(cell == name - tile * TILE).astype(F32).astype(BF) for tile in pair], axis=0
        )
        return jnp.dot(select, value, preferred_element_type=F32)

    order = [0, tiles - 1] + list(range(1, tiles - 1))
    pairs = [order[i : i + 2] for i in range(0, tiles, 2)]
    name = names(1)
    for s in range(SPEC):
        for mask in range(1, half):
            far_copy(s, mask).wait_recv()
        for pair in pairs:
            value = gathered(name, pair, far_in[s].reshape(half * cap, levels)).astype(BF)
            for j, tile in enumerate(pair):
                part_out[s, tile] = value[j * TILE : (j + 1) * TILE]
                part_copy(s, tile).start()
        for masks in groups[s * stride // SPEC : (s + 1) * stride // SPEC]:
            for mask in masks:
                if mask != 0:
                    near_copy(mask).start()
    for mask in range(1, half):
        near_copy(mask).wait_recv()
    name = names(0)
    for pair in pairs:
        value = gathered(name, pair, near_in[...].reshape(half * cap, width))
        for j, tile in enumerate(pair):
            out_ref[tile * TILE : (tile + 1) * TILE, :] = value[j * TILE : (j + 1) * TILE]
    for s in range(SPEC):
        lanes = slice(s * levels, (s + 1) * levels)
        for pair in pairs:
            for tile in pair:
                part_copy(s, tile).wait_recv()
                span = slice(tile * TILE, (tile + 1) * TILE)
                out_ref[span, lanes] = out_ref[span, lanes] + part_in[s, tile].astype(F32)
            if s == SPEC - 1 and pair is pairs[0]:
                edge_out[0] = out_ref[cells - RIM :, :]
                edge_out[1] = out_ref[:RIM, :]
                edge_copy(0).start()
                edge_copy(1).start()
    edge_copy(0).wait_recv()
    edge_copy(1).wait_recv()
    low_ref[...] = jnp.where(me == 0, 0.0, edge_in[0])
    high_ref[...] = jnp.where(me == n - 1, 0.0, edge_in[1])

    for mask in range(1, half):
        cell_copy(mask).wait_send()
        near_copy(mask).wait_send()
        for s in range(SPEC):
            far_copy(s, mask).wait_send()
    for tile in order:
        for s in range(SPEC):
            part_copy(s, tile).wait_send()
    edge_copy(0).wait_send()
    edge_copy(1).wait_send()


def route(hist, dest, cell_in, cells):
    replicas, rows, width = hist.shape
    n, own_n = lax.axis_size(("cell", "own")), lax.axis_size("own")
    half, cap, tiles, levels = n // 2, 2 * rows // n, cells // TILE, width // SPEC
    dma = pltpu.SemaphoreType.DMA
    return pl.pallas_call(
        functools.partial(route_kernel, n, own_n),
        out_shape=(
            jax.ShapeDtypeStruct((cells, width), F32),
            jax.ShapeDtypeStruct((RIM, width), F32),
            jax.ShapeDtypeStruct((RIM, width), F32),
        ),
        in_specs=[pl.BlockSpec(memory_space=pltpu.HBM)] * 3,
        out_specs=(pl.BlockSpec(memory_space=pltpu.VMEM),) * 3,
        scratch_shapes=[
            pltpu.VMEM((replicas, rows, width), BF),
            pltpu.VMEM((1, rows), jnp.int32),
            pltpu.VMEM((1, rows), jnp.int32),
            pltpu.VMEM((rows, width), BF),
            pltpu.VMEM((1, rows), jnp.int32),
            pltpu.VMEM((cap, rows), BF),
            pltpu.VMEM((half, cap, width), BF),
            pltpu.VMEM((half, cap, width), BF),
            pltpu.VMEM((SPEC, half, cap, levels), BF),
            pltpu.VMEM((SPEC, half, cap, levels), BF),
            pltpu.VMEM((half, 2, cap), jnp.int32),
            pltpu.VMEM((half, 2, cap), jnp.int32),
            pltpu.VMEM((SPEC, tiles, TILE, levels), BF),
            pltpu.VMEM((SPEC, tiles, TILE, levels), BF),
            pltpu.VMEM((2, RIM, width), F32),
            pltpu.VMEM((2, RIM, width), F32),
            dma((3,)),
            dma((half,)),
            dma((half,)),
            dma((SPEC, half)),
            dma((SPEC, half)),
            dma((half,)),
            dma((half,)),
            dma((SPEC, tiles)),
            dma((SPEC, tiles)),
            dma((2,)),
            dma((2,)),
        ],
        compiler_params=pltpu.CompilerParams(
            collective_id=0, has_side_effects=True, vmem_limit_bytes=48 * 1024 * 1024
        ),
        name="route",
    )(hist, dest, cell_in)


def body(hist, dest, cell_in, offsets):
    rows = hist.shape[0]
    cellhist, low, high = route(
        jnp.transpose(hist, (1, 0, 2)), dest.reshape(1, rows), cell_in.reshape(1, rows), offsets.shape[1]
    )
    lam, stat = fit(cellhist, low, high, offsets)
    return jnp.transpose(lam, (1, 0, 2)), stat


def solution(mesh):
    placed = (
        P(("cell", "own"), None, None),
        P(("cell", "own"), None),
        P(("cell", "own")),
        P(None, ("cell", "own")),
    )
    return jax.shard_map(
        body,
        mesh=mesh,
        in_specs=placed,
        out_specs=(P(None, None, ("cell", "own")), P(None, ("cell", "own"))),
        check_vma=False,
    )
```

```python
import functools
import jax
import jax.numpy as jnp
import numpy as np
from jax import lax
from jax.experimental import pallas as pl
from jax.experimental.pallas import tpu as pltpu
from jax.sharding import PartitionSpec as P

SPEC = 2
MOM = 6
NEWTON = 8
NEIGH = 4
W = 4
TILE = 256
RIM = 8
BF = jnp.bfloat16
F32 = jnp.float32


def legendre_rows(levels, count):
    xpos = (2.0 * np.arange(levels) + 1.0) / levels - 1.0
    table = [np.ones_like(xpos), xpos]
    for order in range(1, count - 1):
        table.append(((2 * order + 1) * xpos * table[order] - order * table[order - 1]) / (order + 1))
    return np.stack(table, axis=0)


def product_weights(count):
    weights = {}
    for m in range(1, count + 1):
        for n in range(1, m + 1):
            series = np.polynomial.legendre.legmul(np.eye(m + 1)[m], np.eye(n + 1)[n])
            weights[m, n] = [(k, float(v)) for k, v in enumerate(series) if abs(v) > 1e-12]
    return weights


def halves(value):
    high = value.astype(BF)
    return high, (value - high.astype(F32)).astype(BF)


def fit_tables(levels):
    rows = np.zeros((16, levels))
    rows[: 2 * MOM + 1] = legendre_rows(levels, 2 * MOM + 1)
    high = np.asarray(rows, jnp.bfloat16)
    low = np.asarray(rows - high.astype(np.float64), jnp.bfloat16)
    gather = np.zeros((32, 2 * levels), jnp.bfloat16)
    gather[:16, :levels] = high
    gather[:16, levels:] = high
    gather[16:, :levels] = low
    spread = np.zeros((levels, 32), jnp.bfloat16)
    spread[:, 0:MOM] = high[1 : MOM + 1].T
    spread[:, 8 : 8 + MOM] = low[1 : MOM + 1].T
    spread[:, 16 : 16 + MOM] = high[1 : MOM + 1].T
    return jnp.asarray(gather), jnp.asarray(spread)


def fit_kernel(cell_ref, low_ref, high_ref, off_ref, gather_ref, spread_ref, lam_ref, stat_ref,
               ext, target, sums, lam, mu):
    cells = cell_ref.shape[0]
    levels = gather_ref.shape[1] // 2
    tiles = cells // TILE
    span = TILE + 2 * RIM
    ext[0:RIM, :] = low_ref[...]
    ext[RIM : RIM + cells, :] = cell_ref[...]
    ext[RIM + cells :, :] = high_ref[...]
    tn = (((0,), (0,)), ((), ()))

    def moments(value):
        high, low = halves(value)
        both = jnp.dot(gather_ref[...], jnp.concatenate([high, low], axis=0), preferred_element_type=F32)
        return both[:16] + both[16:]

    def exponent(group):
        value = lam[group // tiles, :, group % tiles, :]
        high = value.astype(BF).astype(F32)
        stacked = jnp.concatenate([high, high, value - high, jnp.zeros_like(high)], axis=0)
        return jnp.dot(spread_ref[...], stacked.astype(BF), preferred_element_type=F32)

    place = lax.broadcasted_iota(jnp.int32, (span, TILE), 0) - lax.broadcasted_iota(jnp.int32, (span, TILE), 1) - RIM
    level = lax.broadcasted_iota(jnp.int32, (levels, TILE), 0)
    for block in range(tiles):
        cols = slice(block * TILE, (block + 1) * TILE)
        picker = (place == 0).astype(F32)
        for j in range(NEIGH):
            picker = picker + (place == off_ref[j : j + 1, cols]).astype(F32)
        picker = picker.astype(BF)
        high, low = halves(ext[block * TILE : block * TILE + span, :])
        summed = lax.dot_general(high, picker, tn, preferred_element_type=F32) + lax.dot_general(
            low, picker, tn, preferred_element_type=F32
        )
        for s in range(SPEC):
            field = summed[s * levels : (s + 1) * levels]
            below = jnp.where(level == 0, 0.0, pltpu.roll(field, 1, 0))
            above = jnp.where(level == levels - 1, 0.0, pltpu.roll(field, levels - 1, 0))
            smooth = 1.0 + (0.5 * field + 0.25 * (below + above))
            group = s * tiles + block
            target[group] = smooth
            sums[s, :, block, :] = moments(smooth)
    weights = product_weights(MOM)
    flat = legendre_rows(levels, 2 * MOM + 1).mean(axis=1)
    hess = np.array([
        [sum(v * flat[k] for k, v in weights[max(m, n), min(m, n)]) - flat[m] * flat[n] + 0.01 * (m == n)
         for n in range(1, MOM + 1)]
        for m in range(1, MOM + 1)
    ])
    solved = 0.5 * np.linalg.inv(hess)
    for s in range(SPEC):
        inverse = 1.0 / sums[s, 0]
        for m in range(MOM):
            mu[s, m] = sums[s, m + 1] * inverse
        for m in range(MOM):
            total = jnp.zeros_like(inverse)
            for k in range(MOM):
                if abs(solved[m, k]) > 1e-14:
                    total = total + float(solved[m, k]) * (mu[s, k] - float(flat[k + 1]))
            lam[s, m] = total
        for m in range(MOM, 8):
            lam[s, m] = jnp.zeros_like(inverse)

    def measure(s):
        for block in range(tiles):
            sums[s, :, block, :] = moments(jnp.exp(exponent(s * tiles + block)))

    def update(s):
        inverse = 1.0 / sums[s, 0]
        mean = [None] + [sums[s, k] * inverse for k in range(1, 2 * MOM + 1)]
        raw = [[None] * MOM for _ in range(MOM)]
        unit = [[None] * MOM for _ in range(MOM)]
        scale = [None] * MOM
        for row in range(MOM):
            for col in range(row + 1):
                total = -mean[row + 1] * mean[col + 1]
                if row == col:
                    total = total + 0.01
                for k, v in weights[row + 1, col + 1]:
                    total = total + (v if k == 0 else v * mean[k])
                for inner in range(col):
                    total = total - raw[row][inner] * unit[col][inner]
                if row == col:
                    scale[row] = 1.0 / total
                else:
                    raw[row][col] = total
                    unit[row][col] = total * scale[col]
        forward = []
        for row in range(MOM):
            total = mean[row + 1] - mu[s, row]
            for inner in range(row):
                total = total - unit[row][inner] * forward[inner]
            forward.append(total)
        backward = [None] * MOM
        for row in reversed(range(MOM)):
            total = forward[row] * scale[row]
            for inner in range(row + 1, MOM):
                total = total - unit[inner][row] * backward[inner]
            backward[row] = total
            lam[s, row] = lam[s, row] - 0.5 * total

    measure(0)

    def step(_, carry):
        measure(1)
        update(0)
        measure(0)
        update(1)
        return carry

    lax.fori_loop(1, NEWTON, step, 0)
    for s in range(SPEC):
        for block in range(tiles):
            cols = slice(block * TILE, (block + 1) * TILE)
            group = s * tiles + block
            lam_ref[:, s, cols] = lam[s, 0:MOM, block, :]
            value = exponent(group)
            norm = jnp.log(jnp.sum(jnp.exp(value), axis=0, keepdims=True))
            field = target[group]
            total = jnp.log(jnp.sum(field, axis=0, keepdims=True))
            ratio = (jnp.log(field) - value) + (norm - total)
            stat_ref[s : s + 1, cols] = (2.0 / levels) * jnp.sum(field * ratio, axis=0, keepdims=True)


def fit(cellhist, low, high, offsets):
    cells, width = cellhist.shape
    levels = width // SPEC
    groups = SPEC * cells // TILE
    gather, spread = fit_tables(levels)
    return pl.pallas_call(
        fit_kernel,
        out_shape=(
            jax.ShapeDtypeStruct((MOM, SPEC, cells), F32),
            jax.ShapeDtypeStruct((SPEC, cells), F32),
        ),
        in_specs=[pl.BlockSpec(memory_space=pltpu.VMEM)] * 6,
        out_specs=(pl.BlockSpec(memory_space=pltpu.VMEM),) * 2,
        scratch_shapes=[
            pltpu.VMEM((cells + 2 * RIM, width), F32),
            pltpu.VMEM((groups, levels, TILE), F32),
            pltpu.VMEM((SPEC, 16, groups // SPEC, TILE), F32),
            pltpu.VMEM((SPEC, 8, groups // SPEC, TILE), F32),
            pltpu.VMEM((SPEC, 8, groups // SPEC, TILE), F32),
        ],
        compiler_params=pltpu.CompilerParams(vmem_limit_bytes=32 * 1024 * 1024),
        name="fit",
    )(cellhist, low, high, offsets, gather, spread)


def route_kernel(n, own_n, hist_hbm, dest_hbm, cell_hbm, out_ref, low_ref, high_ref,
                 hist, dest, cell_in, packed, rel, ones, near_out, near_in, far_out, far_in,
                 send_cells, recv_cells, part_out, part_in, edge_out, edge_in,
                 load, near_send, near_recv, far_send, far_recv, cell_send, cell_recv,
                 part_send, part_recv, edge_send, edge_recv):
    half = n // 2
    rows, width = packed.shape
    levels = width // SPEC
    cap = ones.shape[0]
    cells = out_ref.shape[0]
    tiles = cells // TILE
    me = lax.axis_index("cell") * own_n + lax.axis_index("own")
    after, before = lax.rem(me + 1, n), lax.rem(me + n - 1, n)
    bits = [lax.rem(lax.div(me, 1 << b), 2) for b in range(n.bit_length() - 1)]

    def flipped(mask):
        index = me
        for b, bit in enumerate(bits):
            if mask >> b & 1:
                index = index + (1 << b) * (1 - 2 * bit)
        return index

    def place(index):
        return (lax.div(index, own_n), lax.rem(index, own_n))

    def remote(source, target, sent, received, index):
        return pltpu.make_async_remote_copy(
            src_ref=source, dst_ref=target, send_sem=sent, recv_sem=received,
            device_id=place(index), device_id_type=pl.DeviceIdType.MESH)

    def near_copy(mask):
        return remote(near_out.at[mask], near_in.at[mask], near_send.at[mask], near_recv.at[mask], flipped(mask))

    def far_copy(s, mask):
        return remote(far_out.at[s, mask], far_in.at[s, mask], far_send.at[s, mask], far_recv.at[s, mask], flipped(mask))

    def cell_copy(mask):
        return remote(send_cells.at[mask], recv_cells.at[mask], cell_send.at[mask], cell_recv.at[mask], flipped(mask))

    def part_copy(s, tile):
        return remote(part_out.at[s, tile], part_in.at[s, tile], part_send.at[s, tile], part_recv.at[s, tile], flipped(half))

    def edge_copy(side):
        return remote(edge_out.at[side], edge_in.at[side], edge_send.at[side], edge_recv.at[side],
                      after if side == 0 else before)

    loads = [
        pltpu.make_async_copy(dest_hbm, dest, load.at[0]),
        pltpu.make_async_copy(cell_hbm, cell_in, load.at[1]),
        pltpu.make_async_copy(hist_hbm, hist, load.at[2]),
    ]
    for copy in loads:
        copy.start()

    barrier = pltpu.get_barrier_semaphore()
    for index in [flipped(mask) for mask in range(1, half + 1)] + [after, before]:
        pl.semaphore_signal(barrier, inc=1, device_id=place(index), device_id_type=pl.DeviceIdType.MESH)

    loads[0].wait()
    rel[...] = dest[...] ^ me
    loads[1].wait()
    upto = (
        lax.broadcasted_iota(jnp.int32, (TILE, TILE), 0) <= lax.broadcasted_iota(jnp.int32, (TILE, TILE), 1)
    ).astype(F32).astype(BF)
    block = lax.broadcasted_iota(jnp.int32, (n, TILE), 0)
    slot = lax.broadcasted_iota(jnp.int32, (cap, TILE), 0).astype(F32)
    seen = jnp.zeros((n, 1), F32)
    slots = jnp.zeros((2 * n, cap), F32)
    for piece in range(rows // TILE):
        cols = slice(piece * TILE, (piece + 1) * TILE)
        member = (block == rel[:, cols]).astype(F32)
        count = jnp.dot(member.astype(BF), upto, preferred_element_type=F32) + seen
        rank = jnp.sum(member * count, axis=0, keepdims=True) - 1.0
        seen = count[:, TILE - 1 :]
        hot = (slot == rank).astype(F32).astype(BF)
        ones[:, cols] = hot
        cell = cell_in[:, cols]
        major = (cell >> 5).astype(F32)
        minor = (cell & 31).astype(F32)
        named = jnp.concatenate([member * major, member * minor], axis=0).astype(BF)
        slots = slots + lax.dot_general(named, hot, (((1,), (1,)), ((), ())), preferred_element_type=F32)
    numbers = (32.0 * slots[:n] + slots[n:]).astype(jnp.int32)
    send_cells[:, 0, :] = numbers[:half]
    send_cells[:, 1, :] = numbers[half:]
    loads[2].wait()
    packed[...] = (hist[0].astype(F32) + hist[1].astype(F32) + hist[2].astype(F32)).astype(BF)

    def pack(kind, masks):
        chosen = [(rel[...] == kind * half + mask).astype(F32).astype(BF) for mask in masks]
        picked = jnp.concatenate([ones[...] * row for row in chosen], axis=0)
        return jnp.dot(picked, packed[...], preferred_element_type=F32).astype(BF)

    stride = half // 4
    groups = [[q + j * stride for j in range(4)] for q in sorted(range(stride), key=lambda q: (q % 2, -q))]

    pl.semaphore_wait(barrier, half + 2)
    for masks in groups:
        value = pack(1, masks)
        for j, mask in enumerate(masks):
            for s in range(SPEC):
                piece = value[j * cap : (j + 1) * cap, s * levels : (s + 1) * levels]
                if mask == 0:
                    far_in[s, mask] = piece
                else:
                    far_out[s, mask] = piece
            if mask != 0:
                far_copy(0, mask).start()
        for mask in masks:
            if mask != 0:
                cell_copy(mask).start()
    for masks in groups:
        for mask in masks:
            if mask != 0:
                far_copy(1, mask).start()
    recv_cells[0] = send_cells[0]
    for masks in groups:
        value = pack(0, masks)
        for j, mask in enumerate(masks):
            piece = value[j * cap : (j + 1) * cap]
            if mask == 0:
                near_in[mask] = piece
            else:
                near_out[mask] = piece

    for mask in range(1, half):
        cell_copy(mask).wait_recv()

    def names(kind):
        return jnp.concatenate([recv_cells[mask, kind : kind + 1, :] for mask in range(half)], axis=1)

    def gathered(name, pair, value):
        cell = lax.broadcasted_iota(jnp.int32, (TILE, half * cap), 0)
        select = jnp.concatenate(
            [(cell == name - tile * TILE).astype(F32).astype(BF) for tile in pair], axis=0
        )
        return jnp.dot(select, value, preferred_element_type=F32)

    order = [0, tiles - 1] + list(range(1, tiles - 1))
    pairs = [order[i : i + 2] for i in range(0, tiles, 2)]
    name = names(1)
    for s in range(SPEC):
        for mask in range(1, half):
            far_copy(s, mask).wait_recv()
        for pair in pairs:
            value = gathered(name, pair, far_in[s].reshape(half * cap, levels)).astype(BF)
            for j, tile in enumerate(pair):
                part_out[s, tile] = value[j * TILE : (j + 1) * TILE]
                part_copy(s, tile).start()
        for masks in groups[s * stride // SPEC : (s + 1) * stride // SPEC]:
            for mask in masks:
                if mask != 0:
                    near_copy(mask).start()
    for mask in range(1, half):
        near_copy(mask).wait_recv()
    name = names(0)
    for pair in pairs:
        value = gathered(name, pair, near_in[...].reshape(half * cap, width))
        for j, tile in enumerate(pair):
            out_ref[tile * TILE : (tile + 1) * TILE, :] = value[j * TILE : (j + 1) * TILE]
    for s in range(SPEC):
        lanes = slice(s * levels, (s + 1) * levels)
        for pair in pairs:
            for tile in pair:
                part_copy(s, tile).wait_recv()
                span = slice(tile * TILE, (tile + 1) * TILE)
                out_ref[span, lanes] = out_ref[span, lanes] + part_in[s, tile].astype(F32)
            if s == SPEC - 1 and pair is pairs[0]:
                edge_out[0] = out_ref[cells - RIM :, :]
                edge_out[1] = out_ref[:RIM, :]
                edge_copy(0).start()
                edge_copy(1).start()
    edge_copy(0).wait_recv()
    edge_copy(1).wait_recv()
    low_ref[...] = jnp.where(me == 0, 0.0, edge_in[0])
    high_ref[...] = jnp.where(me == n - 1, 0.0, edge_in[1])

    for mask in range(1, half):
        cell_copy(mask).wait_send()
        near_copy(mask).wait_send()
        for s in range(SPEC):
            far_copy(s, mask).wait_send()
    for tile in order:
        for s in range(SPEC):
            part_copy(s, tile).wait_send()
    edge_copy(0).wait_send()
    edge_copy(1).wait_send()


def route(hist, dest, cell_in, cells):
    replicas, rows, width = hist.shape
    n, own_n = lax.axis_size(("cell", "own")), lax.axis_size("own")
    half, cap, tiles, levels = n // 2, 2 * rows // n, cells // TILE, width // SPEC
    dma = pltpu.SemaphoreType.DMA
    return pl.pallas_call(
        functools.partial(route_kernel, n, own_n),
        out_shape=(
            jax.ShapeDtypeStruct((cells, width), F32),
            jax.ShapeDtypeStruct((RIM, width), F32),
            jax.ShapeDtypeStruct((RIM, width), F32),
        ),
        in_specs=[pl.BlockSpec(memory_space=pltpu.HBM)] * 3,
        out_specs=(pl.BlockSpec(memory_space=pltpu.VMEM),) * 3,
        scratch_shapes=[
            pltpu.VMEM((replicas, rows, width), BF),
            pltpu.VMEM((1, rows), jnp.int32),
            pltpu.VMEM((1, rows), jnp.int32),
            pltpu.VMEM((rows, width), BF),
            pltpu.VMEM((1, rows), jnp.int32),
            pltpu.VMEM((cap, rows), BF),
            pltpu.VMEM((half, cap, width), BF),
            pltpu.VMEM((half, cap, width), BF),
            pltpu.VMEM((SPEC, half, cap, levels), BF),
            pltpu.VMEM((SPEC, half, cap, levels), BF),
            pltpu.VMEM((half, 2, cap), jnp.int32),
            pltpu.VMEM((half, 2, cap), jnp.int32),
            pltpu.VMEM((SPEC, tiles, TILE, levels), BF),
            pltpu.VMEM((SPEC, tiles, TILE, levels), BF),
            pltpu.VMEM((2, RIM, width), F32),
            pltpu.VMEM((2, RIM, width), F32),
            dma((3,)),
            dma((half,)),
            dma((half,)),
            dma((SPEC, half)),
            dma((SPEC, half)),
            dma((half,)),
            dma((half,)),
            dma((SPEC, tiles)),
            dma((SPEC, tiles)),
            dma((2,)),
            dma((2,)),
        ],
        compiler_params=pltpu.CompilerParams(
            collective_id=0, has_side_effects=True, vmem_limit_bytes=63 * 1024 * 1024
        ),
        name="route",
    )(hist, dest, cell_in)


def body(hist, dest, cell_in, offsets):
    rows = hist.shape[0]
    cellhist, low, high = route(
        jnp.transpose(hist, (1, 0, 2)), dest.reshape(1, rows), cell_in.reshape(1, rows), offsets.shape[1]
    )
    lam, stat = fit(cellhist, low, high, offsets)
    return jnp.transpose(lam, (1, 0, 2)), stat


def solution(mesh):
    placed = (
        P(("cell", "own"), None, None),
        P(("cell", "own"), None),
        P(("cell", "own")),
        P(None, ("cell", "own")),
    )
    return jax.shard_map(
        body,
        mesh=mesh,
        in_specs=placed,
        out_specs=(P(None, None, ("cell", "own")), P(None, ("cell", "own"))),
        check_vma=False,
    )
```

```python
import functools
import jax
import jax.numpy as jnp
import numpy as np
from jax import lax
from jax.experimental import pallas as pl
from jax.experimental.pallas import tpu as pltpu
from jax.sharding import PartitionSpec as P

SPEC = 2
MOM = 6
NEWTON = 8
NEIGH = 4
W = 4
TILE = 256
RIM = 8
BF = jnp.bfloat16
F32 = jnp.float32


def legendre_rows(levels, count):
    xpos = (2.0 * np.arange(levels) + 1.0) / levels - 1.0
    table = [np.ones_like(xpos), xpos]
    for order in range(1, count - 1):
        table.append(((2 * order + 1) * xpos * table[order] - order * table[order - 1]) / (order + 1))
    return np.stack(table, axis=0)


def product_weights(count):
    weights = {}
    for m in range(1, count + 1):
        for n in range(1, m + 1):
            series = np.polynomial.legendre.legmul(np.eye(m + 1)[m], np.eye(n + 1)[n])
            weights[m, n] = [(k, float(v)) for k, v in enumerate(series) if abs(v) > 1e-12]
    return weights


def halves(value):
    high = value.astype(BF)
    return high, (value - high.astype(F32)).astype(BF)


def fit_tables(levels):
    rows = np.zeros((16, levels))
    rows[: 2 * MOM + 1] = legendre_rows(levels, 2 * MOM + 1)
    high = np.asarray(rows, jnp.bfloat16)
    low = np.asarray(rows - high.astype(np.float64), jnp.bfloat16)
    gather = np.zeros((32, 2 * levels), jnp.bfloat16)
    gather[:16, :levels] = high
    gather[:16, levels:] = high
    gather[16:, :levels] = low
    spread = np.zeros((levels, 32), jnp.bfloat16)
    spread[:, 0:MOM] = high[1 : MOM + 1].T
    spread[:, 8 : 8 + MOM] = low[1 : MOM + 1].T
    spread[:, 16 : 16 + MOM] = high[1 : MOM + 1].T
    return jnp.asarray(gather), jnp.asarray(spread)


def fit_kernel(cell_ref, low_ref, high_ref, off_ref, gather_ref, spread_ref, lam_ref, stat_ref,
               ext, target, sums, lam, mu):
    cells = cell_ref.shape[0]
    levels = gather_ref.shape[1] // 2
    tiles = cells // TILE
    span = TILE + 2 * RIM
    ext[0:RIM, :] = low_ref[...]
    ext[RIM : RIM + cells, :] = cell_ref[...]
    ext[RIM + cells :, :] = high_ref[...]
    tn = (((0,), (0,)), ((), ()))

    def moments(value):
        high, low = halves(value)
        both = jnp.dot(gather_ref[...], jnp.concatenate([high, low], axis=0), preferred_element_type=F32)
        return both[:16] + both[16:]

    def exponent(group):
        value = lam[group // tiles, :, group % tiles, :]
        high = value.astype(BF).astype(F32)
        stacked = jnp.concatenate([high, high, value - high, jnp.zeros_like(high)], axis=0)
        return jnp.dot(spread_ref[...], stacked.astype(BF), preferred_element_type=F32)

    place = lax.broadcasted_iota(jnp.int32, (span, TILE), 0) - lax.broadcasted_iota(jnp.int32, (span, TILE), 1) - RIM
    level = lax.broadcasted_iota(jnp.int32, (levels, TILE), 0)
    for block in range(tiles):
        cols = slice(block * TILE, (block + 1) * TILE)
        picker = (place == 0).astype(F32)
        for j in range(NEIGH):
            picker = picker + (place == off_ref[j : j + 1, cols]).astype(F32)
        picker = picker.astype(BF)
        high, low = halves(ext[block * TILE : block * TILE + span, :])
        summed = lax.dot_general(high, picker, tn, preferred_element_type=F32) + lax.dot_general(
            low, picker, tn, preferred_element_type=F32
        )
        for s in range(SPEC):
            field = summed[s * levels : (s + 1) * levels]
            below = jnp.where(level == 0, 0.0, pltpu.roll(field, 1, 0))
            above = jnp.where(level == levels - 1, 0.0, pltpu.roll(field, levels - 1, 0))
            smooth = 1.0 + (0.5 * field + 0.25 * (below + above))
            group = s * tiles + block
            target[group] = smooth
            sums[s, :, block, :] = moments(smooth)
    weights = product_weights(MOM)
    flat = legendre_rows(levels, 2 * MOM + 1).mean(axis=1)
    hess = np.array([
        [sum(v * flat[k] for k, v in weights[max(m, n), min(m, n)]) - flat[m] * flat[n] + 0.01 * (m == n)
         for n in range(1, MOM + 1)]
        for m in range(1, MOM + 1)
    ])
    solved = 0.5 * np.linalg.inv(hess)
    for s in range(SPEC):
        inverse = 1.0 / sums[s, 0]
        for m in range(MOM):
            mu[s, m] = sums[s, m + 1] * inverse
        for m in range(MOM):
            total = jnp.zeros_like(inverse)
            for k in range(MOM):
                if abs(solved[m, k]) > 1e-14:
                    total = total + float(solved[m, k]) * (mu[s, k] - float(flat[k + 1]))
            lam[s, m] = total
        for m in range(MOM, 8):
            lam[s, m] = jnp.zeros_like(inverse)

    def measure(s):
        for block in range(tiles):
            sums[s, :, block, :] = moments(jnp.exp(exponent(s * tiles + block)))

    def update(s):
        inverse = 1.0 / sums[s, 0]
        mean = [None] + [sums[s, k] * inverse for k in range(1, 2 * MOM + 1)]
        raw = [[None] * MOM for _ in range(MOM)]
        unit = [[None] * MOM for _ in range(MOM)]
        scale = [None] * MOM
        for row in range(MOM):
            for col in range(row + 1):
                total = -mean[row + 1] * mean[col + 1]
                if row == col:
                    total = total + 0.01
                for k, v in weights[row + 1, col + 1]:
                    total = total + (v if k == 0 else v * mean[k])
                for inner in range(col):
                    total = total - raw[row][inner] * unit[col][inner]
                if row == col:
                    scale[row] = 1.0 / total
                else:
                    raw[row][col] = total
                    unit[row][col] = total * scale[col]
        forward = []
        for row in range(MOM):
            total = mean[row + 1] - mu[s, row]
            for inner in range(row):
                total = total - unit[row][inner] * forward[inner]
            forward.append(total)
        backward = [None] * MOM
        for row in reversed(range(MOM)):
            total = forward[row] * scale[row]
            for inner in range(row + 1, MOM):
                total = total - unit[inner][row] * backward[inner]
            backward[row] = total
            lam[s, row] = lam[s, row] - 0.5 * total

    measure(0)

    def step(_, carry):
        measure(1)
        update(0)
        measure(0)
        update(1)
        return carry

    lax.fori_loop(1, NEWTON, step, 0)
    for s in range(SPEC):
        for block in range(tiles):
            cols = slice(block * TILE, (block + 1) * TILE)
            group = s * tiles + block
            lam_ref[:, s, cols] = lam[s, 0:MOM, block, :]
            value = exponent(group)
            norm = jnp.log(jnp.sum(jnp.exp(value), axis=0, keepdims=True))
            field = target[group]
            total = jnp.log(jnp.sum(field, axis=0, keepdims=True))
            ratio = (jnp.log(field) - value) + (norm - total)
            stat_ref[s : s + 1, cols] = (2.0 / levels) * jnp.sum(field * ratio, axis=0, keepdims=True)


def fit(cellhist, low, high, offsets):
    cells, width = cellhist.shape
    levels = width // SPEC
    groups = SPEC * cells // TILE
    gather, spread = fit_tables(levels)
    return pl.pallas_call(
        fit_kernel,
        out_shape=(
            jax.ShapeDtypeStruct((MOM, SPEC, cells), F32),
            jax.ShapeDtypeStruct((SPEC, cells), F32),
        ),
        in_specs=[pl.BlockSpec(memory_space=pltpu.VMEM)] * 6,
        out_specs=(pl.BlockSpec(memory_space=pltpu.VMEM),) * 2,
        scratch_shapes=[
            pltpu.VMEM((cells + 2 * RIM, width), F32),
            pltpu.VMEM((groups, levels, TILE), F32),
            pltpu.VMEM((SPEC, 16, groups // SPEC, TILE), F32),
            pltpu.VMEM((SPEC, 8, groups // SPEC, TILE), F32),
            pltpu.VMEM((SPEC, 8, groups // SPEC, TILE), F32),
        ],
        compiler_params=pltpu.CompilerParams(vmem_limit_bytes=32 * 1024 * 1024),
        name="fit",
    )(cellhist, low, high, offsets, gather, spread)


def route_kernel(n, own_n, hist_hbm, dest_hbm, cell_hbm, out_ref, low_ref, high_ref,
                 hist, dest, cell_in, packed, rel, ones, near_out, near_in, far_out, far_in,
                 send_cells, recv_cells, part_out, part_in, edge_out, edge_in,
                 load, near_send, near_recv, far_send, far_recv, cell_send, cell_recv,
                 part_send, part_recv, edge_send, edge_recv):
    half = n // 2
    rows, width = packed.shape
    levels = width // SPEC
    cap = ones.shape[0]
    cells = out_ref.shape[0]
    tiles = cells // TILE
    me = lax.axis_index("cell") * own_n + lax.axis_index("own")
    after, before = lax.rem(me + 1, n), lax.rem(me + n - 1, n)
    bits = [lax.rem(lax.div(me, 1 << b), 2) for b in range(n.bit_length() - 1)]

    def flipped(mask):
        index = me
        for b, bit in enumerate(bits):
            if mask >> b & 1:
                index = index + (1 << b) * (1 - 2 * bit)
        return index

    def place(index):
        return (lax.div(index, own_n), lax.rem(index, own_n))

    def remote(source, target, sent, received, index):
        return pltpu.make_async_remote_copy(
            src_ref=source, dst_ref=target, send_sem=sent, recv_sem=received,
            device_id=place(index), device_id_type=pl.DeviceIdType.MESH)

    def near_copy(mask):
        return remote(near_out.at[mask], near_in.at[mask], near_send.at[mask], near_recv.at[mask], flipped(mask))

    def far_copy(s, mask):
        return remote(far_out.at[s, mask], far_in.at[s, mask], far_send.at[s, mask], far_recv.at[s, mask], flipped(mask))

    def cell_copy(mask):
        return remote(send_cells.at[mask], recv_cells.at[mask], cell_send.at[mask], cell_recv.at[mask], flipped(mask))

    def part_copy(s, tile):
        return remote(part_out.at[s, tile], part_in.at[s, tile], part_send.at[s, tile], part_recv.at[s, tile], flipped(half))

    def edge_copy(side):
        return remote(edge_out.at[side], edge_in.at[side], edge_send.at[side], edge_recv.at[side],
                      after if side == 0 else before)

    loads = [
        pltpu.make_async_copy(dest_hbm, dest, load.at[0]),
        pltpu.make_async_copy(cell_hbm, cell_in, load.at[1]),
        pltpu.make_async_copy(hist_hbm, hist, load.at[2]),
    ]
    for copy in loads:
        copy.start()

    barrier = pltpu.get_barrier_semaphore()
    for index in [flipped(mask) for mask in range(1, half + 1)] + [after, before]:
        pl.semaphore_signal(barrier, inc=1, device_id=place(index), device_id_type=pl.DeviceIdType.MESH)

    loads[0].wait()
    rel[...] = dest[...] ^ me
    loads[1].wait()
    upto = (
        lax.broadcasted_iota(jnp.int32, (TILE, TILE), 0) <= lax.broadcasted_iota(jnp.int32, (TILE, TILE), 1)
    ).astype(F32).astype(BF)
    block = lax.broadcasted_iota(jnp.int32, (n, TILE), 0)
    slot = lax.broadcasted_iota(jnp.int32, (cap, TILE), 0).astype(F32)
    seen = jnp.zeros((n, 1), F32)
    slots = jnp.zeros((2 * n, cap), F32)
    for piece in range(rows // TILE):
        cols = slice(piece * TILE, (piece + 1) * TILE)
        member = (block == rel[:, cols]).astype(F32)
        count = jnp.dot(member.astype(BF), upto, preferred_element_type=F32) + seen
        rank = jnp.sum(member * count, axis=0, keepdims=True) - 1.0
        seen = count[:, TILE - 1 :]
        hot = (slot == rank).astype(F32).astype(BF)
        ones[:, cols] = hot
        cell = cell_in[:, cols]
        major = (cell >> 5).astype(F32)
        minor = (cell & 31).astype(F32)
        named = jnp.concatenate([member * major, member * minor], axis=0).astype(BF)
        slots = slots + lax.dot_general(named, hot, (((1,), (1,)), ((), ())), preferred_element_type=F32)
    numbers = (32.0 * slots[:n] + slots[n:]).astype(jnp.int32)
    send_cells[:, 0, :] = numbers[:half]
    send_cells[:, 1, :] = numbers[half:]
    loads[2].wait()
    packed[...] = (hist[0].astype(F32) + hist[1].astype(F32) + hist[2].astype(F32)).astype(BF)

    def pack(kind, masks):
        chosen = [(rel[...] == kind * half + mask).astype(F32).astype(BF) for mask in masks]
        picked = jnp.concatenate([ones[...] * row for row in chosen], axis=0)
        return jnp.dot(picked, packed[...], preferred_element_type=F32).astype(BF)

    stride = half // 4
    groups = [[q + j * stride for j in range(4)] for q in sorted(range(stride), key=lambda q: (q % 2, -q))]

    pl.semaphore_wait(barrier, half + 2)
    for masks in groups:
        value = pack(1, masks)
        for j, mask in enumerate(masks):
            for s in range(SPEC):
                piece = value[j * cap : (j + 1) * cap, s * levels : (s + 1) * levels]
                if mask == 0:
                    far_in[s, mask] = piece
                else:
                    far_out[s, mask] = piece
            if mask != 0:
                far_copy(0, mask).start()
        for mask in masks:
            if mask != 0:
                cell_copy(mask).start()
    for masks in groups:
        for mask in masks:
            if mask != 0:
                far_copy(1, mask).start()
    recv_cells[0] = send_cells[0]
    for masks in groups:
        value = pack(0, masks)
        for j, mask in enumerate(masks):
            piece = value[j * cap : (j + 1) * cap]
            if mask == 0:
                near_in[mask] = piece
            else:
                near_out[mask] = piece

    for mask in range(1, half):
        cell_copy(mask).wait_recv()

    def names(kind):
        return jnp.concatenate([recv_cells[mask, kind : kind + 1, :] for mask in range(half)], axis=1)

    def gathered(name, pair, value):
        cell = lax.broadcasted_iota(jnp.int32, (TILE, half * cap), 0)
        select = jnp.concatenate(
            [(cell == name - tile * TILE).astype(F32).astype(BF) for tile in pair], axis=0
        )
        return jnp.dot(select, value, preferred_element_type=F32)

    order = [0, tiles - 1] + list(range(1, tiles - 1))
    pairs = [order[i : i + 2] for i in range(0, tiles, 2)]
    name = names(1)
    for s in range(SPEC):
        for mask in range(1, half):
            far_copy(s, mask).wait_recv()
        for pair in pairs:
            value = gathered(name, pair, far_in[s].reshape(half * cap, levels)).astype(BF)
            for j, tile in enumerate(pair):
                part_out[s, tile] = value[j * TILE : (j + 1) * TILE]
                part_copy(s, tile).start()
        for masks in groups[s * stride // SPEC : (s + 1) * stride // SPEC]:
            for mask in masks:
                if mask != 0:
                    near_copy(mask).start()
    for mask in range(1, half):
        near_copy(mask).wait_recv()
    name = names(0)
    for pair in pairs:
        value = gathered(name, pair, near_in[...].reshape(half * cap, width))
        for j, tile in enumerate(pair):
            out_ref[tile * TILE : (tile + 1) * TILE, :] = value[j * TILE : (j + 1) * TILE]
    for s in range(SPEC):
        lanes = slice(s * levels, (s + 1) * levels)
        for pair in pairs:
            for tile in pair:
                part_copy(s, tile).wait_recv()
                span = slice(tile * TILE, (tile + 1) * TILE)
                out_ref[span, lanes] = out_ref[span, lanes] + part_in[s, tile].astype(F32)
            if s == SPEC - 1 and pair is pairs[0]:
                edge_out[0] = out_ref[cells - RIM :, :]
                edge_out[1] = out_ref[:RIM, :]
                edge_copy(0).start()
                edge_copy(1).start()
    edge_copy(0).wait_recv()
    edge_copy(1).wait_recv()
    low_ref[...] = jnp.where(me == 0, 0.0, edge_in[0])
    high_ref[...] = jnp.where(me == n - 1, 0.0, edge_in[1])

    for mask in range(1, half):
        cell_copy(mask).wait_send()
        near_copy(mask).wait_send()
        for s in range(SPEC):
            far_copy(s, mask).wait_send()
    for tile in order:
        for s in range(SPEC):
            part_copy(s, tile).wait_send()
    edge_copy(0).wait_send()
    edge_copy(1).wait_send()


def route(hist, dest, cell_in, cells):
    replicas, rows, width = hist.shape
    n, own_n = lax.axis_size(("cell", "own")), lax.axis_size("own")
    half, cap, tiles, levels = n // 2, 2 * rows // n, cells // TILE, width // SPEC
    dma = pltpu.SemaphoreType.DMA
    return pl.pallas_call(
        functools.partial(route_kernel, n, own_n),
        out_shape=(
            jax.ShapeDtypeStruct((cells, width), F32),
            jax.ShapeDtypeStruct((RIM, width), F32),
            jax.ShapeDtypeStruct((RIM, width), F32),
        ),
        in_specs=[pl.BlockSpec(memory_space=pltpu.HBM)] * 3,
        out_specs=(pl.BlockSpec(memory_space=pltpu.VMEM),) * 3,
        scratch_shapes=[
            pltpu.VMEM((replicas, rows, width), BF),
            pltpu.VMEM((1, rows), jnp.int32),
            pltpu.VMEM((1, rows), jnp.int32),
            pltpu.VMEM((rows, width), BF),
            pltpu.VMEM((1, rows), jnp.int32),
            pltpu.VMEM((cap, rows), BF),
            pltpu.VMEM((half, cap, width), BF),
            pltpu.VMEM((half, cap, width), BF),
            pltpu.VMEM((SPEC, half, cap, levels), BF),
            pltpu.VMEM((SPEC, half, cap, levels), BF),
            pltpu.VMEM((half, 2, cap), jnp.int32),
            pltpu.VMEM((half, 2, cap), jnp.int32),
            pltpu.VMEM((SPEC, tiles, TILE, levels), BF),
            pltpu.VMEM((SPEC, tiles, TILE, levels), BF),
            pltpu.VMEM((2, RIM, width), F32),
            pltpu.VMEM((2, RIM, width), F32),
            dma((3,)),
            dma((half,)),
            dma((half,)),
            dma((SPEC, half)),
            dma((SPEC, half)),
            dma((half,)),
            dma((half,)),
            dma((SPEC, tiles)),
            dma((SPEC, tiles)),
            dma((2,)),
            dma((2,)),
        ],
        compiler_params=pltpu.CompilerParams(
            collective_id=0, has_side_effects=True, vmem_limit_bytes=61 * 1024 * 1024 + 512 * 1024
        ),
        name="route",
    )(hist, dest, cell_in)


def body(hist, dest, cell_in, offsets):
    rows = hist.shape[0]
    cellhist, low, high = route(
        jnp.transpose(hist, (1, 0, 2)), dest.reshape(1, rows), cell_in.reshape(1, rows), offsets.shape[1]
    )
    lam, stat = fit(cellhist, low, high, offsets)
    return jnp.transpose(lam, (1, 0, 2)), stat


def solution(mesh):
    placed = (
        P(("cell", "own"), None, None),
        P(("cell", "own"), None),
        P(("cell", "own")),
        P(None, ("cell", "own")),
    )
    return jax.shard_map(
        body,
        mesh=mesh,
        in_specs=placed,
        out_specs=(P(None, None, ("cell", "own")), P(None, ("cell", "own"))),
        check_vma=False,
    )
```
